256 devices in a mesh: dp: 8 (over y, core), seq: 32 (over z, x).
Axes of the slice: x: 4, y: 4, z: 8, core: 2. Of those that a mesh axis runs over, the one named last changes fastest.
Arguments:
- point_rows: float32 [262144, 512], P(('dp', 'seq')), may hold values from -6 to 6
- serial_order: int32 [8, 32768], P('dp', 'seq'), may hold values from 0 to 32767, as said below
- scene_counts: int32 [8, 64], P('dp'), may hold values from 1 to 1024, 32768 in all within a row
- pool_counts: int32 [8, 32, 512], P('dp', 'seq'), may hold values from 1 to 3, 1024 in all within a row
- conv_gain: float32 [512], replicated, may hold values from 0.5 to 1.5
- conv_kernel: float32 [7, 512], replicated, may hold values from -2.5 to 2.5
- mixer_gain: float32 [512], replicated, may hold values from 0.5 to 1.5
- weight_in: bfloat16 [512, 2048], replicated, may hold values from -0.25 to 0.25
- weight_out: bfloat16 [2048, 512], replicated, may hold values from -0.125 to 0.125
- grad_out: float32 [131072, 512], P(('dp', 'seq')), may hold values from -6 to 6
Outputs:
- mixed_rows: float32 [131072, 512], P(('dp', 'seq'))
- grad_rows: float32 [262144, 512], P(('dp', 'seq'))
- grad_weight_in: float32 [512, 2048], P(None, 'seq')
- grad_weight_out: float32 [2048, 512], P('seq')
- grad_kernel: float32 [7, 512], replicated
- grad_conv_gain: float32 [512], replicated
- grad_mixer_gain: float32 [512], replicated
The draws below stay inside these ranges and needn't reach their ends.
Inputs may be any that keep to these rules, and one draw needn't show every extreme that they name: `serial_order`: each row is a permutation of the group's rows. The 1024 serialized positions of one device take at most 48 rows from any one device's block of 1024 rows, and exactly 48 from some device.
All inputs are finite; a program needn't handle non-finite values.
Results may differ from the reference program's by a relative error of at most 0.0055.
Values sent between devices are 32-bit elements; how exact they have to be, the bound alone decides.
A program may use at most 128 MiB of HBM per device.

```python
import math
import jax
import jax.numpy as jnp
import numpy as np
from jax import lax

C = 512
H = 2048
KS = 7
P_DEV = 1024
SEGS = 512
TOTAL = 32768
ROWS = 262144
POOLED = 131072
SCENES = 64
N_DP = 8
N_SEQ = 32


def serial_group(key, seq_count, row_count):
    block_rows = row_count // (2 * seq_count)
    key_first, key_second, key_rotate, key_slots, key_rows = jax.random.split(key, 5)
    first_off = jax.random.randint(key_first, (), 0, seq_count)
    second_off = (first_off + 1 + jax.random.randint(key_second, (), 0, seq_count - 1)) % seq_count
    offsets = jnp.arange(2 * seq_count, dtype=jnp.int32) // 2
    offsets = offsets.at[2 * second_off + 1].set(first_off)
    rotate = jax.random.permutation(key_rotate, seq_count).astype(jnp.int32)
    slot_order = jax.vmap(lambda subkey: jax.random.permutation(subkey, row_count))(jax.random.split(key_slots, seq_count)).astype(jnp.int32)
    row_order = jax.vmap(lambda subkey: jax.random.permutation(subkey, row_count))(jax.random.split(key_rows, seq_count)).astype(jnp.int32)
    block_ids = slot_order // block_rows
    within = slot_order % block_rows
    source = (rotate[:, None] + offsets[block_ids]) % seq_count
    local_row = row_order[source, block_ids * block_rows + within]
    return (source * row_count + local_row).reshape(-1).astype(jnp.int32)


def draw_serial_order(key, part):
    key = jax.random.fold_in(key, 7)
    groups = ROWS // TOTAL
    seq_count = TOTAL // P_DEV
    group_keys = jax.random.split(key, groups)
    return jax.vmap(lambda subkey: serial_group(subkey, seq_count, P_DEV))(group_keys)


def block_scale(own_key, extent, cuts, smallest, high):
    gain, own = 1.0, jax.random.fold_in(own_key, 6)
    for position, blocks in cuts:
        heights = jnp.exp(jax.random.uniform(jax.random.fold_in(own, position), (blocks,), jnp.float32, smallest / len(cuts), high / len(cuts)))
        gain = gain * jnp.repeat(heights, extent[position] // blocks).reshape([-1 if axis == position else 1 for axis in range(len(extent))])
    return gain


def split_up(number_of, total, limit, slope):
    weights = [(1 << 20) // math.isqrt(standing ** slope) + 1 for standing in range(2, number_of + 1)]
    surplus, given = total - limit - (number_of - 1), [1] * (number_of - 1)
    while surplus > 0:
        candidates = [i for i in range(number_of - 1) if given[i] < limit]
        mass, remaining = sum([weights[i] for i in candidates]), surplus
        for i in candidates:
            addition = min(limit - given[i], max(1, remaining * weights[i] // mass), surplus)
            given[i] = given[i] + addition
            surplus = surplus - addition
    return np.array([limit] + given)


def ragged(stream_key, count, total, reach, skew):
    if count == 2:
        one = jax.random.randint(stream_key, (), max(1, total - reach), min(reach, total - 1) + 1)
        return jnp.stack([one, total - one])
    sizes = jnp.asarray(split_up(count, total, reach, skew), jnp.int32)
    pairs = (count - 1) // 2
    donor, receiver = sizes[1:1 + 2 * pairs:2], sizes[2:2 + 2 * pairs:2]
    slack = jnp.minimum(donor - 1, reach - receiver)
    passed = jax.random.randint(jax.random.fold_in(stream_key, 1), (pairs,), 0, 1 << 20) % (slack + 1)
    sizes = sizes.at[1:1 + 2 * pairs:2].set(donor - passed).at[2:2 + 2 * pairs:2].set(receiver + passed)
    return sizes[jax.random.permutation(jax.random.fold_in(stream_key, 2), count)]


def centred(stream_key, dims, scale, reach, cuts=(), kind=jnp.bfloat16):
    drawn = scale * jax.random.normal(stream_key, dims, jnp.float32)
    if cuts:
        drawn = drawn * block_scale(stream_key, dims, cuts, -0.22, 0.18)
    return jnp.clip(drawn, -reach, reach).astype(kind)


def setup_inputs(seed: int = 0) -> dict:
    seeds = jax.random.split(jax.random.key(seed), 11)
    point_rows = centred(seeds[0], (ROWS, C), 1.0, 6.0, ((0, 256),), jnp.float32)
    serial_order = draw_serial_order(jax.random.fold_in(seeds[10], 71), 0)
    scene_counts = jax.vmap(lambda own: ragged(own, SCENES, TOTAL, P_DEV, 2))(jax.random.split(seeds[2], N_DP)).reshape((N_DP, SCENES)).astype(jnp.int32)
    pool_counts = jax.vmap(lambda own: ragged(own, SEGS, P_DEV, 3, 0))(jax.random.split(seeds[3], N_DP * N_SEQ)).reshape((N_DP, N_SEQ, SEGS)).astype(jnp.int32)
    conv_gain = jnp.clip(1.0 + 0.1 * jax.random.normal(seeds[4], (C,), jnp.float32), 0.5, 1.5)
    conv_kernel = centred(seeds[5], (KS, C), 0.4, 2.5, (), jnp.float32)
    mixer_gain = jnp.clip(1.0 + 0.1 * jax.random.normal(seeds[6], (C,), jnp.float32), 0.5, 1.5)
    weight_in = centred(seeds[7], (C, H), C ** -0.5, 0.25)
    weight_out = centred(seeds[8], (H, C), H ** -0.5, 0.125)
    grad_out = centred(seeds[9], (POOLED, C), 1.0, 6.0, ((0, 256),), jnp.float32)
    return {"point_rows": point_rows, "serial_order": serial_order, "scene_counts": scene_counts, "pool_counts": pool_counts, "conv_gain": conv_gain, "conv_kernel": conv_kernel, "mixer_gain": mixer_gain, "weight_in": weight_in, "weight_out": weight_out, "grad_out": grad_out}


NORM_EPS = 1e-05

def layer_norm(values, gain_vec):
    centre = values - lax.optimization_barrier(jnp.mean(values, axis=-1, keepdims=True))
    spread = lax.optimization_barrier(jnp.mean(centre * centre, axis=-1, keepdims=True))
    return centre * lax.rsqrt(spread + NORM_EPS) * gain_vec

def conv_block(serial, gain_vec, kernel, scene_ids):
    row_count = serial.shape[0]
    half_width = kernel.shape[0] // 2
    normed_pad = jnp.pad(layer_norm(serial, gain_vec), ((half_width, half_width), (0, 0)))
    padded_ids = jnp.pad(scene_ids, (half_width, half_width), constant_values=-1)
    conved = serial
    for offset in range(kernel.shape[0]):
        same_scene = (padded_ids[offset:offset + row_count] == scene_ids).astype(jnp.float32)
        conved = conved + kernel[offset] * same_scene[:, None] * normed_pad[offset:offset + row_count]
    return conved

def mixer_forward(pooled, gain_vec, weight_in, weight_out):
    normed = layer_norm(pooled, gain_vec).astype(jnp.bfloat16)
    hidden = jnp.dot(normed, weight_in, preferred_element_type=jnp.float32)
    active = jax.nn.gelu(hidden).astype(jnp.bfloat16)
    mixed_rows = pooled + jnp.dot(active, weight_out, preferred_element_type=jnp.float32)
    return (normed, hidden, active, mixed_rows)

def mixer_backward(pooled, gain_vec, weight_in, weight_out, normed, hidden, active, grad_mixed):
    grad_low = grad_mixed.astype(jnp.bfloat16)
    first_dims = (((0,), (0,)), ((), ()))
    last_dims = (((1,), (1,)), ((), ()))
    grad_wout = lax.dot_general(active, grad_low, first_dims, preferred_element_type=jnp.float32)
    grad_active = lax.dot_general(grad_low, weight_out, last_dims, preferred_element_type=jnp.float32)
    grad_hidden = jax.vjp(jax.nn.gelu, hidden)[1](grad_active)[0].astype(jnp.bfloat16)
    grad_win = lax.dot_general(normed, grad_hidden, first_dims, preferred_element_type=jnp.float32)
    grad_normed = lax.dot_general(grad_hidden, weight_in, last_dims, preferred_element_type=jnp.float32)
    back_fn = jax.vjp(layer_norm, pooled, gain_vec)[1]
    grad_ln_in, grad_gain = back_fn(grad_normed)
    return (grad_mixed + grad_ln_in, grad_gain, grad_win, grad_wout)

def reference(point_rows, serial_order, scene_counts, pool_counts, conv_gain, conv_kernel, mixer_gain, weight_in, weight_out, grad_out):
    mixed_parts = []
    grad_parts = []
    grad_win = jnp.zeros((C, H), jnp.float32)
    grad_wout = jnp.zeros((H, C), jnp.float32)
    grad_kern = jnp.zeros((KS, C), jnp.float32)
    grad_cgain = jnp.zeros((C,), jnp.float32)
    grad_mgain = jnp.zeros((C,), jnp.float32)
    positions = jnp.arange(TOTAL, dtype=jnp.int32)
    inside = jnp.arange(P_DEV, dtype=jnp.int32)
    for group_idx in range(N_DP):
        group_rows = point_rows[group_idx * TOTAL:(group_idx + 1) * TOTAL]
        group_order = serial_order[group_idx]
        serial = group_rows[group_order]
        scene_ends = jnp.cumsum(scene_counts[group_idx])
        scene_ids = lax.optimization_barrier(jnp.sum((positions[:, None] >= scene_ends[None, :]).astype(jnp.int32), axis=1))
        conved, conv_back = jax.vjp(lambda rows_in, gain_in, kern_in: conv_block(rows_in, gain_in, kern_in, scene_ids), serial, conv_gain, conv_kernel)
        local_ends = jnp.cumsum(pool_counts[group_idx], axis=1)
        local_ids = lax.optimization_barrier(jnp.sum((inside[None, :, None] >= local_ends[:, None, :]).astype(jnp.int32), axis=2))
        pool_ids = (local_ids + jnp.arange(N_SEQ, dtype=jnp.int32)[:, None] * SEGS).reshape(-1)
        lengths = pool_counts[group_idx].reshape(-1).astype(jnp.float32)[:, None]
        pooled = jax.ops.segment_sum(conved, pool_ids, num_segments=N_SEQ * SEGS) / lengths
        normed, hidden, active, mixed_rows = mixer_forward(pooled, mixer_gain, weight_in, weight_out)
        mixed_parts.append(mixed_rows)
        grad_mixed = grad_out[group_idx * N_SEQ * SEGS:(group_idx + 1) * N_SEQ * SEGS]
        grad_pooled, part_mgain, part_win, part_wout = mixer_backward(pooled, mixer_gain, weight_in, weight_out, normed, hidden, active, grad_mixed)
        grad_conved = (grad_pooled / lengths)[pool_ids]
        grad_serial, part_cgain, part_kern = conv_back(grad_conved)
        grad_parts.append(jnp.zeros_like(group_rows).at[group_order].set(grad_serial))
        grad_win = grad_win + part_win
        grad_wout = grad_wout + part_wout
        grad_kern = grad_kern + part_kern
        grad_cgain = grad_cgain + part_cgain
        grad_mgain = grad_mgain + part_mgain
    return (jnp.concatenate(mixed_parts, axis=0), jnp.concatenate(grad_parts, axis=0), grad_win, grad_wout, grad_kern, grad_cgain, grad_mgain)
```

```python
import jax
import jax.numpy as jnp
from jax import lax
from jax.experimental import pallas as pl
from jax.experimental.pallas import tpu as pltpu
from jax.sharding import PartitionSpec as P

NORM_EPS = 1e-05
MESH = pl.DeviceIdType.MESH
f32, bf16 = jnp.float32, jnp.bfloat16
NX = 4
CH = 32
PAD = 8
GELU_A = 0.7978845608028654
GELU_B = 0.044715


def iota_f(shape, dim):
    return lax.broadcasted_iota(jnp.int32, shape, dim).astype(f32)


def ones_where(mask):
    return jnp.where(mask, 1.0, 0.0)


def split_hi_lo(value):
    high = value.astype(bf16)
    return high, (value - high.astype(f32)).astype(bf16)


def mm(a, b):
    return jnp.dot(a, b, preferred_element_type=f32)


def mm_last(a, b):
    return lax.dot_general(a, b, (((1,), (1,)), ((), ())), preferred_element_type=f32)


def mm_first(a, b):
    return lax.dot_general(a, b, (((0,), (0,)), ((), ())), preferred_element_type=f32)


def fold8(value):
    return jnp.sum(value.reshape(value.shape[0] // 8, 8, value.shape[1]), axis=0)


def rows_from(window, offset, count):
    size = window.shape[0]
    return pltpu.roll(window, (size - offset) % size, 0)[0:count]


def wide(value):
    return jnp.concatenate([value] * 4, axis=1)


def kernel(
    n_dp, n_seq, cap,
    rows_hbm, order_ref, scene_ref, pool_ref, cgain_ref, taps_ref, mgain_ref, win_hbm, wout_hbm, gout_hbm,
    mixed_hbm, grows_hbm, gwin_ref, gwout_ref, gtaps_ref, gcg_ref, gmg_ref,
    rows_v, rows_hi, rows_lo, list_s, list_r, kmat, scol, srow, tcol, pick,
    outb, inb, inb2, ser, xhat, rstd, sid, val_hi, val_lo,
    pool_m, pool_t, plen, gout_v, glow, mixed_v, xhat2, norm2, gnorm, rstd2,
    win_v, wout_v, gw, rc, ry, wx, rx, wz, rz, fin, gc, gtap_acc, small, rs1, rs2, rs3,
    ld_sem, idx_s, idx_r, row_s, row_r, back_s, back_r, halo_s, halo_r,
    core_s, core_r, y_s, y_r, x_s, x_r, z_s, z_r, s1_s, s1_r, s2_s, s2_r, s3_s, s3_r, f_s, f_r,
):
    count, chans = rows_v.shape
    segs = mixed_v.shape[0]
    hidden = wout_v.shape[0]
    n_y, n_z = n_dp // 2, n_seq // NX
    group = 8
    n_groups = n_seq // group
    slots = group * cap
    dp, me = lax.axis_index("dp"), lax.axis_index("seq")
    y, core = lax.div(dp, 2), lax.rem(dp, 2)
    z, x = lax.div(me, NX), lax.rem(me, NX)
    my_group = lax.div(me, group)

    def remote(src, dst, send, recv, to_dp, to_seq):
        return pltpu.make_async_remote_copy(
            src_ref=src, dst_ref=dst, send_sem=send, recv_sem=recv,
            device_id=(to_dp, to_seq), device_id_type=MESH,
        )

    def each(n, fn, start=0):
        def step(i, carry):
            fn(i)
            return carry
        lax.fori_loop(start, n, step, 0)

    loads = [
        pltpu.make_async_copy(rows_hbm, rows_v, ld_sem.at[0]),
        pltpu.make_async_copy(win_hbm, win_v, ld_sem.at[1]),
        pltpu.make_async_copy(wout_hbm, wout_v, ld_sem.at[2]),
        pltpu.make_async_copy(gout_hbm, gout_v, ld_sem.at[3]),
    ]
    for load in loads:
        load.start()

    barrier = pltpu.get_barrier_semaphore()
    each(n_seq, lambda i: pl.semaphore_signal(
        barrier, inc=1, device_id=(dp, lax.rem(me + i, n_seq)), device_id_type=MESH), 1)
    each(n_dp, lambda i: pl.semaphore_signal(
        barrier, inc=1, device_id=(lax.rem(dp + i, n_dp), me), device_id_type=MESH), 1)

    order = order_ref[...]
    shift = count.bit_length() - 1
    owner = (order >> shift).astype(f32)
    local = order & (count - 1)
    local_hi = (local >> 5).astype(f32)
    local_lo = (local & 31).astype(f32)
    owner_col = jnp.transpose(jnp.broadcast_to(owner, (128, count)))
    lane = iota_f((128, 128), 1)
    below = ones_where(iota_f((128, 128), 0) > lane).astype(bf16)
    before = jnp.zeros((1, 128), f32)
    for b in range(count // 128):
        own_b = owner_col[b * 128:(b + 1) * 128]
        hot = ones_where(own_b == lane)
        ranks = mm(below, hot.astype(bf16)) + before
        before = before + jnp.sum(hot, axis=0, keepdims=True)
        rank = jnp.broadcast_to(jnp.sum(hot * ranks, axis=1, keepdims=True), (128, 128))
        scol[b * 128:(b + 1) * 128, :] = own_b * cap + rank
        kmat[b * 128:(b + 1) * 128, :] = ones_where(rank == lane).astype(bf16)
    srow[...] = jnp.transpose(scol[...])[0:8, :]
    owner_hot = ones_where(jnp.broadcast_to(owner, (n_seq, count)) == iota_f((n_seq, count), 0))
    kval = kmat[...]
    lists = (
        mm((owner_hot * local_hi).astype(bf16), kval) * 32.0
        + mm((owner_hot * local_lo).astype(bf16), kval)
        + mm(owner_hot.astype(bf16), kval)
        - 1.0
    )
    for p in range(n_seq):
        list_s[p] = jnp.broadcast_to(lists[p:p + 1, :], (8, 128))
    list_r[me] = list_s[me]

    pl.semaphore_wait(barrier, n_seq - 1 + n_dp - 1)

    def send_list(i):
        p = lax.rem(me + i, n_seq)
        return remote(list_s.at[p], list_r.at[me], idx_s.at[p], idx_r.at[me], dp, p)

    def recv_list(i):
        p = lax.rem(me + i, n_seq)
        return remote(list_s.at[p], list_r.at[p], idx_s.at[p], idx_r.at[p], dp, p)

    each(n_seq, lambda i: send_list(i).start(), 1)

    loads[0].wait()

    def split_rows(i):
        at = pl.ds(pl.multiple_of(i * CH, CH), CH)
        rows_hi[at, :], rows_lo[at, :] = split_hi_lo(rows_v[at, :])

    each(count // CH, split_rows)
    each(n_seq, lambda i: recv_list(i).wait_recv(), 1)

    tcol[...] = jnp.transpose(list_r[...].reshape(n_seq * 8, 128))

    def row_out(p, src, dst, send, recv):
        return remote(src.at[p], dst.at[me], send.at[p], recv.at[me], dp, p)

    def row_self(src, dst, recv):
        return pltpu.make_async_copy(src.at[me], dst.at[me], recv.at[me])

    def launch(p0, dst, send, recv):
        def one(i):
            p = p0 + i

            @pl.when(p != me)
            def _():
                row_out(p, outb, dst, send, recv).start()

            @pl.when(p == me)
            def _():
                row_self(outb, dst, recv).start()
        each(group, one)

    def arrive(p0, dst, send, recv):
        def one(i):
            p = p0 + i

            @pl.when(p != me)
            def _():
                remote(outb.at[p], dst.at[p], send.at[p], recv.at[p], dp, p).wait_recv()

            @pl.when(p == me)
            def _():
                row_self(outb, dst, recv).wait()
        each(group, one)

    def group_out(g):
        return group * lax.rem(my_group + g, n_groups)

    def group_in(g):
        return group * lax.rem(my_group + n_groups - g, n_groups)

    tlane = lax.broadcasted_iota(jnp.int32, (cap, n_seq * 8), 1)
    rlane = iota_f((cap, count), 1)

    def gather_group(g):
        p0 = group_out(g)

        def one(i):
            p = p0 + i
            col = jnp.sum(jnp.where(tlane == p * 8, tcol[0:cap, :], 0.0), axis=1, keepdims=True)
            pick[pl.ds(pl.multiple_of(p * cap, 16), cap), :] = ones_where(
                jnp.broadcast_to(col, (cap, count)) == rlane).astype(bf16)
        each(group, one)
        hot = pick[pl.ds(pl.multiple_of(p0 * cap, 16), slots), :]
        made = mm(hot, rows_hi[...]) + mm(hot, rows_lo[...])
        outb[pl.ds(p0, group)] = made.reshape(group, cap, chans)
        launch(p0, inb, row_s, row_r)

    each(n_groups, gather_group)

    scene_n = scene_ref.shape[1]
    upto = ones_where(iota_f((scene_n, scene_n), 0) <= iota_f((scene_n, scene_n), 1))
    scene_ends = lax.dot_general(
        jnp.broadcast_to(scene_ref[...].astype(f32), (8, scene_n)), upto, (((1,), (0,)), ((), ())),
        precision=lax.Precision.HIGHEST, preferred_element_type=f32)[0:1, :]
    first_pos = (me * count - PAD).astype(f32)

    def scenes(i):
        start = pl.multiple_of(i * 8, 8)
        pos = iota_f((8, scene_n), 0) + (first_pos + start.astype(f32))
        ids = jnp.sum(ones_where(pos >= scene_ends), axis=1, keepdims=True)
        ids = jnp.where(pos[:, 0:1] < 0.0, -1.0, ids)
        sid[pl.ds(start, 8), :] = jnp.broadcast_to(ids, (8, 128))

    each(sid.shape[0] // 8, scenes)

    lens = jnp.broadcast_to(pool_ref[...].astype(f32), (128, segs))
    len_col = jnp.transpose(lens)
    plen[...] = len_col
    tri_rows, tri_cols = iota_f((segs, segs), 0), iota_f((segs, segs), 1)
    end_col = mm(ones_where(tri_cols <= tri_rows).astype(bf16), len_col.astype(bf16))
    end_row = mm(lens[0:8].astype(bf16), ones_where(tri_rows <= tri_cols).astype(bf16))[0:1, :]
    start_col = end_col - len_col
    start_row = end_row - lens[0:1]
    for t in range(count // 128):
        at_pos = iota_f((segs, 128), 1) + float(t * 128)
        pool_m[:, t * 128:(t + 1) * 128] = ones_where((at_pos >= start_col) & (at_pos < end_col)).astype(bf16)

    def pool_rows(i):
        start = pl.multiple_of(i * CH, CH)
        at_pos = iota_f((CH, segs), 0) + start.astype(f32)
        pool_t[pl.ds(start, CH), :] = ones_where((at_pos >= start_row) & (at_pos < end_row)).astype(bf16)

    each(count // CH, pool_rows)

    def clear(i):
        ser[pl.ds(pl.multiple_of(i * 8 + PAD, 8), 8), :] = jnp.zeros((8, chans), f32)

    each(count // 8, clear)
    gtap_acc[...] = jnp.zeros(gtap_acc.shape, f32)

    slane = iota_f((count, 128), 1)

    def place_group(g):
        p0 = group_in(g)
        arrive(p0, inb, row_s, row_r)
        high, low = split_hi_lo(inb[pl.ds(p0, group)].reshape(slots, chans))
        at_slot = scol[...] - (p0 * cap).astype(f32)
        hot = jnp.concatenate(
            [ones_where(at_slot == slane + float(128 * t)).astype(bf16) for t in range(slots // 128)], axis=1)
        ser[pl.ds(PAD, count), :] += mm(hot, high) + mm(hot, low)

    each(n_groups, place_group)

    right, left = lax.rem(me + 1, n_seq), lax.rem(me + n_seq - 1, n_seq)

    def halo(buf, k):
        return (
            remote(buf.at[pl.ds(count, PAD)], buf.at[pl.ds(0, PAD)], halo_s.at[k], halo_r.at[k], dp, right),
            remote(buf.at[pl.ds(PAD, PAD)], buf.at[pl.ds(count + PAD, PAD)], halo_s.at[k + 1], halo_r.at[k + 1],
                   dp, left),
        )

    for copy in halo(ser, 0):
        copy.start()

    inv = 1.0 / chans

    def norm_rows(start, rows):
        at = pl.ds(start, rows)
        v = ser[at, :]
        centre = v - jnp.sum(v, axis=1, keepdims=True) * inv
        r = lax.rsqrt(jnp.sum(centre * centre, axis=1, keepdims=True) * inv + NORM_EPS)
        xhat[at, :] = centre * r
        rstd[at, :] = jnp.broadcast_to(r, (rows, 128))

    each(count // CH, lambda i: norm_rows(pl.multiple_of(i * CH + PAD, 8), CH))
    half = taps_ref.shape[0] // 2
    taps = taps_ref[...]
    cgain = cgain_ref[...]
    taps_gain = taps * cgain

    def conv_rows(i):
        base = pl.multiple_of(i * CH, CH)
        here = sid[pl.ds(base + PAD, CH), :]
        total = ser[pl.ds(base + PAD, CH), :]
        around = xhat[pl.ds(base, CH + 2 * PAD), :]
        for d in range(2 * half + 1):
            same = wide(ones_where(sid[pl.ds(base + PAD + d - half, CH), :] == here))
            total = total + taps_gain[d:d + 1, :] * (same * rows_from(around, PAD + d - half, CH))
        at = pl.ds(base, CH)
        val_hi[at, :], val_lo[at, :] = split_hi_lo(total)

    n_chunks = count // CH
    each(n_chunks - 1, conv_rows, 1)
    for copy in halo(ser, 0):
        copy.wait_recv()
    norm_rows(0, PAD)
    norm_rows(count + PAD, PAD)
    each(2, lambda i: conv_rows(i * (n_chunks - 1)))

    mixed_v[...] = mm(pool_m[...], val_hi[...]) + mm(pool_m[...], val_lo[...])
    mgain = mgain_ref[...]
    loads[3].wait()

    def norm_pooled(i):
        at = pl.ds(pl.multiple_of(i * CH, CH), CH)
        v = mixed_v[at, :] / wide(plen[at, :])
        centre = v - jnp.sum(v, axis=1, keepdims=True) * inv
        r = lax.rsqrt(jnp.sum(centre * centre, axis=1, keepdims=True) * inv + NORM_EPS)
        unit = centre * r
        mixed_v[at, :] = v
        xhat2[at, :] = unit
        norm2[at, :] = (unit * mgain).astype(bf16)
        rstd2[at, :] = jnp.broadcast_to(r, (CH, 128))
        glow[at, :] = gout_v[at, :].astype(bf16)
        gnorm[at, :] = jnp.zeros((CH, chans), f32)

    each(segs // CH, norm_pooled)
    loads[1].wait()
    loads[2].wait()

    hb = 512
    n_hb = hidden // hb
    n_cols = chans // 128
    partner = dp + 1 - 2 * core

    def core_copy(j):
        at = pl.ds(pl.multiple_of(j * hb, hb), hb)
        return remote(gw.at[1 - core, :, at, :], rc.at[:, at, :], core_s.at[j], core_r.at[j], partner, me)

    def mlp_block(j):
        at_h = pl.ds(pl.multiple_of(j * hb, hb), hb)
        w_in, w_out = win_v[:, at_h], wout_v[at_h, :]
        n2, gl = norm2[...], glow[...]
        rows_v[0:segs, :] = mm(n2, w_in)
        rows_v[segs:2 * segs, :] = mm_last(gl, w_out)

        def act(i):
            start = pl.multiple_of(i * 16, 16)
            at, at2 = pl.ds(start, 16), pl.ds(start + segs, 16)
            h, ga = rows_v[at, :], rows_v[at2, :]
            h2 = h * h
            t = jnp.tanh(h * (GELU_A + (GELU_A * GELU_B) * h2))
            half_t = 0.5 + 0.5 * t
            slope = half_t + (0.5 * h) * (1.0 - t * t) * (GELU_A + (3.0 * GELU_A * GELU_B) * h2)
            rows_hi[at, :] = (h * half_t).astype(bf16)
            rows_hi[at2, :] = (ga * slope).astype(bf16)

        each(segs // 16, act)
        active, gh = rows_hi[0:segs, :], rows_hi[segs:2 * segs, :]
        mixed_v[...] += mm(active, w_out)
        gnorm[...] += mm_last(gh, w_in)
        part_in, part_out = mm_first(gh, n2), mm_first(active, gl)
        for c in range(n_cols):
            gw[0, c, at_h, :] = part_in[:, c * 128:(c + 1) * 128]
            gw[1, c, at_h, :] = part_out[:, c * 128:(c + 1) * 128]
        core_copy(j).start()

    each(n_hb, mlp_block)
    store_mixed = pltpu.make_async_copy(mixed_v, mixed_hbm, ld_sem.at[4])
    store_mixed.start()

    small[...] = jnp.zeros(small.shape, f32)

    def norm_back(i):
        at = pl.ds(pl.multiple_of(i * CH, CH), CH)
        g, unit = gnorm[at, :], xhat2[at, :]
        prod = g * unit
        small[...] += fold8(prod)
        dx = g * mgain
        a = jnp.sum(dx, axis=1, keepdims=True) * inv
        b = jnp.sum(prod * mgain, axis=1, keepdims=True) * inv
        gp = gout_v[at, :] + wide(rstd2[at, :]) * (dx - a - unit * b)
        rows_hi[at, :], rows_lo[at, :] = split_hi_lo(gp / wide(plen[at, :]))

    each(segs // CH, norm_back)
    mgain_part = jnp.sum(small[...], axis=0, keepdims=True)
    gc[pl.ds(PAD, count), :] = mm(pool_t[...], rows_hi[0:segs, :]) + mm(pool_t[...], rows_lo[0:segs, :])
    for copy in halo(gc, 2):
        copy.start()

    per = 256
    n_per = hidden // per

    def add_core(i):
        c, k = lax.div(i, n_per), lax.rem(i, n_per)
        at = pl.ds(pl.multiple_of(k * per, per), per)
        gw[core, c, at, :] += rc[c, at, :]

    each(n_hb, lambda j: core_copy(j).wait_recv())
    each(n_cols * n_per, add_core)

    def y_send(o):
        yy = lax.rem(y + o, n_y)
        return remote(gw.at[core, yy], ry.at[o - 1], y_s.at[o - 1], y_r.at[o - 1], yy * 2 + core, me)

    each(n_y, lambda o: y_send(o).start(), 1)

    def back_rows(i):
        base = pl.multiple_of(i * CH, CH)
        own = pl.ds(base + PAD, CH)
        here, unit = sid[own, :], xhat[own, :]
        gl = jnp.zeros((CH, chans), f32)
        around = gc[pl.ds(base, CH + 2 * PAD), :]
        for e in range(-half, half + 1):
            same = wide(ones_where(sid[pl.ds(base + PAD + e, CH), :] == here)) * rows_from(around, PAD + e, CH)
            gl = gl + taps[half - e:half - e + 1, :] * same
            gtap_acc[half - e] += fold8(unit * same)
        dx = gl * cgain
        a = jnp.sum(dx, axis=1, keepdims=True) * inv
        b = jnp.sum(dx * unit, axis=1, keepdims=True) * inv
        gs = gc[own, :] + wide(rstd[own, :]) * (dx - a - unit * b)
        at = pl.ds(base, CH)
        val_hi[at, :], val_lo[at, :] = split_hi_lo(gs)

    each(n_chunks - 1, back_rows, 1)
    for copy in halo(gc, 2):
        copy.wait_recv()
    each(2, lambda i: back_rows(i * (n_chunks - 1)))

    def sent_all(i):
        p = lax.rem(me + i, n_seq)
        row_out(p, outb, inb, row_s, row_r).wait_send()

    each(n_seq, sent_all, 1)
    slot_at = iota_f((slots, count), 0)

    def return_group(g):
        p0 = group_out(g)
        hot = ones_where(slot_at == srow[0:1, :] - (p0 * cap).astype(f32)).astype(bf16)
        made = mm(hot, val_hi[...]) + mm(hot, val_lo[...])
        outb[pl.ds(p0, group)] = made.reshape(group, cap, chans)
        launch(p0, inb2, back_s, back_r)

    each(n_groups, return_group)

    for d in range(2 * half + 1):
        small[d:d + 1, :] = jnp.sum(gtap_acc[d], axis=0, keepdims=True)
    small[7:8, :] = mgain_part
    rs1[dp] = small[...]

    def s1_send(o):
        to = lax.rem(dp + o, n_dp)
        return remote(small, rs1.at[dp], s1_s.at[to], s1_r.at[dp], to, me)

    def s1_recv(o):
        to = lax.rem(dp + o, n_dp)
        return remote(small, rs1.at[to], s1_s.at[to], s1_r.at[to], to, me)

    each(n_dp, lambda o: s1_send(o).start(), 1)

    each(n_y, lambda o: y_send(o).wait_recv(), 1)

    def add_y(i):
        zz = lax.div(i, NX)
        xx = lax.rem(i, NX)
        at = pl.ds(pl.multiple_of(i * 64, 64), 64)
        total = gw[core, y, at, :]
        for o in range(n_y - 1):
            total = total + ry[o, at, :]
        wx[xx, zz] = total

    each(n_z * NX, add_y)
    each(n_dp, lambda o: s1_recv(o).wait_recv(), 1)
    total = rs1[0]
    for i in range(1, n_dp):
        total = total + rs1[i]
    rs2[x] = total

    def x_send(o):
        xx = lax.rem(x + o, NX)
        return remote(wx.at[xx], rx.at[o - 1], x_s.at[o - 1], x_r.at[o - 1], dp, z * NX + xx)

    def s2_send(o):
        xx = lax.rem(x + o, NX)
        return remote(rs2.at[x], rs2.at[x], s2_s.at[xx], s2_r.at[x], dp, z * NX + xx)

    def s2_recv(o):
        xx = lax.rem(x + o, NX)
        return remote(rs2.at[x], rs2.at[xx], s2_s.at[xx], s2_r.at[xx], dp, z * NX + xx)

    each(NX, lambda o: x_send(o).start(), 1)
    each(NX, lambda o: s2_send(o).start(), 1)
    each(NX, lambda o: x_send(o).wait_recv(), 1)

    def add_x(zz):
        total = wx[x, zz]
        for o in range(NX - 1):
            total = total + rx[o, zz]
        wz[zz] = total

    each(n_z, add_x)
    each(NX, lambda o: s2_recv(o).wait_recv(), 1)
    total = rs2[0]
    for i in range(1, NX):
        total = total + rs2[i]
    rs3[z] = total

    def z_send(o):
        zz = lax.rem(z + o, n_z)
        return remote(wz.at[zz], rz.at[o - 1], z_s.at[o - 1], z_r.at[o - 1], dp, zz * NX + x)

    def s3_send(o):
        zz = lax.rem(z + o, n_z)
        return remote(rs3.at[z], rs3.at[z], s3_s.at[zz], s3_r.at[z], dp, zz * NX + x)

    def s3_recv(o):
        zz = lax.rem(z + o, n_z)
        return remote(rs3.at[z], rs3.at[zz], s3_s.at[zz], s3_r.at[zz], dp, zz * NX + x)

    each(n_z, lambda o: z_send(o).start(), 1)
    each(n_z, lambda o: s3_send(o).start(), 1)
    each(n_z, lambda o: z_send(o).wait_recv(), 1)
    total = wz[z]
    for o in range(n_z - 1):
        total = total + rz[o]
    fin[core, y] = total

    def f_send(o):
        to = lax.rem(dp + o, n_dp)
        return remote(fin.at[core, y], fin.at[core, y], f_s.at[to], f_r.at[dp], to, me)

    def f_recv(o):
        to = lax.rem(dp + o, n_dp)
        part = fin.at[lax.rem(to, 2), lax.div(to, 2)]
        return remote(fin.at[core, y], part, f_s.at[to], f_r.at[to], to, me)

    each(n_dp, lambda o: f_send(o).start(), 1)
    each(n_z, lambda o: s3_recv(o).wait_recv(), 1)
    total = rs3[0]
    for i in range(1, n_z):
        total = total + rs3[i]
    gtaps_ref[...] = total[0:2 * half + 1, :] * cgain
    gcg_ref[...] = jnp.sum(total[0:2 * half + 1, :] * taps, axis=0, keepdims=True)
    gmg_ref[...] = total[7:8, :]

    def clear_rows(i):
        rows_v[pl.ds(pl.multiple_of(i * 8, 8), 8), :] = jnp.zeros((8, chans), f32)

    each(count // 8, clear_rows)

    def settle_group(g):
        p0 = group_in(g)
        arrive(p0, inb2, back_s, back_r)
        high, low = split_hi_lo(inb2[pl.ds(p0, group)].reshape(slots, chans))
        hot = pick[pl.ds(pl.multiple_of(p0 * cap, 16), slots), :]
        rows_v[...] += mm_first(hot, high) + mm_first(hot, low)

    each(n_groups, settle_group)
    store_rows = pltpu.make_async_copy(rows_v, grows_hbm, ld_sem.at[5])
    store_rows.start()

    each(n_dp, lambda o: f_recv(o).wait_recv(), 1)
    gwout_ref[...] = jnp.concatenate([fin[1, c] for c in range(n_cols)], axis=1)
    for c in range(n_cols):
        piece = jnp.concatenate([fin[0, c], jnp.zeros((64, 128), f32)], axis=0)
        gwin_ref[c * 128:(c + 1) * 128, :] = jnp.transpose(piece)[:, 0:64]

    each(n_seq, lambda i: send_list(i).wait_send(), 1)

    def back_sent(i):
        p = lax.rem(me + i, n_seq)
        row_out(p, outb, inb2, back_s, back_r).wait_send()

    each(n_seq, back_sent, 1)
    for copy in halo(ser, 0) + halo(gc, 2):
        copy.wait_send()
    each(n_hb, lambda j: core_copy(j).wait_send())
    each(n_y, lambda o: y_send(o).wait_send(), 1)
    each(NX, lambda o: x_send(o).wait_send(), 1)
    each(n_z, lambda o: z_send(o).wait_send(), 1)
    each(n_dp, lambda o: s1_send(o).wait_send(), 1)
    each(NX, lambda o: s2_send(o).wait_send(), 1)
    each(n_z, lambda o: s3_send(o).wait_send(), 1)
    each(n_dp, lambda o: f_send(o).wait_send(), 1)
    store_mixed.wait()
    store_rows.wait()


def make_body(n_dp, n_seq):
    n_y, n_z = n_dp // 2, n_seq // NX

    def body(point_rows, serial_order, scene_counts, pool_counts, conv_gain, conv_kernel, mixer_gain,
             weight_in, weight_out, grad_out):
        count, chans = point_rows.shape
        segs = grad_out.shape[0]
        hidden = weight_out.shape[0]
        cap = 3 * (count // (2 * n_seq))
        share = hidden // n_seq
        pads = count + 2 * PAD
        cols = chans // 128
        V = pltpu.VMEM
        D = lambda n: pltpu.SemaphoreType.DMA((n,))
        any_spec = pl.BlockSpec(memory_space=pl.ANY)
        vmem = pl.BlockSpec(memory_space=pltpu.VMEM)
        shape = jax.ShapeDtypeStruct
        scratch = [
            V((count, chans), f32), V((count, chans), bf16), V((count, chans), bf16),
            V((n_seq, 8, 128), f32), V((n_seq, 8, 128), f32), V((count, 128), bf16),
            V((count, 128), f32), V((8, count), f32), V((128, n_seq * 8), f32), V((n_seq * cap, count), bf16),
            V((n_seq, cap, chans), f32), V((n_seq, cap, chans), f32), V((n_seq, cap, chans), f32),
            V((pads, chans), f32), V((pads, chans), f32), V((pads, 128), f32), V((pads, 128), f32),
            V((count, chans), bf16), V((count, chans), bf16),
            V((segs, count), bf16), V((count, segs), bf16), V((segs, 128), f32),
            V((segs, chans), f32), V((segs, chans), bf16), V((segs, chans), f32), V((segs, chans), f32),
            V((segs, chans), bf16), V((segs, chans), f32), V((segs, 128), f32),
            V((chans, hidden), bf16), V((hidden, chans), bf16),
            V((2, cols, hidden, 128), f32), V((cols, hidden, 128), f32), V((n_y - 1, hidden, 128), f32),
            V((NX, n_z, share, 128), f32), V((NX - 1, n_z, share, 128), f32),
            V((n_z, share, 128), f32), V((n_z - 1, share, 128), f32), V((2, cols, share, 128), f32),
            V((pads, chans), f32), V((8, 8, chans), f32), V((8, chans), f32),
            V((n_dp, 8, chans), f32), V((NX, 8, chans), f32), V((n_z, 8, chans), f32),
            D(6), D(n_seq), D(n_seq), D(n_seq), D(n_seq), D(n_seq), D(n_seq), D(4), D(4),
            D(hidden // 512), D(hidden // 512), D(n_y), D(n_y), D(NX), D(NX), D(n_z), D(n_z),
            D(n_dp), D(n_dp), D(NX), D(NX), D(n_z), D(n_z), D(n_dp), D(n_dp),
        ]
        outs = pl.pallas_call(
            lambda *refs: kernel(n_dp, n_seq, cap, *refs),
            out_shape=(
                shape((segs, chans), f32), shape((count, chans), f32), shape((chans, share), f32),
                shape((share, chans), f32), shape(conv_kernel.shape, f32), shape((1, chans), f32),
                shape((1, chans), f32),
            ),
            in_specs=[any_spec] + [vmem] * 6 + [any_spec] * 3,
            out_specs=(any_spec, any_spec, vmem, vmem, vmem, vmem, vmem),
            scratch_shapes=scratch,
            compiler_params=pltpu.CompilerParams(
                collective_id=0, has_side_effects=True, vmem_limit_bytes=62 * 1024 * 1024),
            name="point_window",
        )(
            point_rows, serial_order, scene_counts, pool_counts.reshape(1, segs), conv_gain[None], conv_kernel,
            mixer_gain[None], weight_in, weight_out, grad_out,
        )
        mixed, grows, gwin, gwout, gtaps, gcg, gmg = outs
        return mixed, grows, gwin, gwout, gtaps, gcg[0], gmg[0]

    return body


def solution(mesh):
    return jax.shard_map(
        make_body(mesh.shape["dp"], mesh.shape["seq"]),
        mesh=mesh,
        in_specs=(
            P(("dp", "seq"), None), P("dp", "seq"), P("dp", None), P("dp", "seq", None), P(), P(), P(), P(), P(),
            P(("dp", "seq"), None),
        ),
        out_specs=(
            P(("dp", "seq"), None), P(("dp", "seq"), None), P(None, "seq"), P("seq", None), P(), P(), P(),
        ),
        check_vma=False,
    )
```

```python
import jax
import jax.numpy as jnp
from jax import lax
from jax.experimental import pallas as pl
from jax.experimental.pallas import tpu as pltpu
from jax.sharding import PartitionSpec as P

NORM_EPS = 1e-05
MESH = pl.DeviceIdType.MESH
f32, bf16 = jnp.float32, jnp.bfloat16
NX = 4
CH = 32
PAD = 8
GELU_A = 0.7978845608028654
GELU_B = 0.044715


def iota_f(shape, dim):
    return lax.broadcasted_iota(jnp.int32, shape, dim).astype(f32)


def ones_where(mask):
    return jnp.where(mask, 1.0, 0.0)


def split_hi_lo(value):
    high = value.astype(bf16)
    return high, (value - high.astype(f32)).astype(bf16)


def mm(a, b):
    return jnp.dot(a, b, preferred_element_type=f32)


def mm_last(a, b):
    return lax.dot_general(a, b, (((1,), (1,)), ((), ())), preferred_element_type=f32)


def mm_first(a, b):
    return lax.dot_general(a, b, (((0,), (0,)), ((), ())), preferred_element_type=f32)


def fold8(value):
    return jnp.sum(value.reshape(value.shape[0] // 8, 8, value.shape[1]), axis=0)


def rows_from(window, offset, count):
    size = window.shape[0]
    return pltpu.roll(window, (size - offset) % size, 0)[0:count]


def wide(value):
    return jnp.concatenate([value] * 4, axis=1)


def kernel(
    n_dp, n_seq, cap, spare,
    rows_hbm, order_ref, scene_ref, pool_ref, cgain_ref, taps_ref, mgain_ref, win_hbm, wout_hbm, gout_hbm,
    mixed_hbm, grows_hbm, gwin_ref, gwout_ref, gtaps_ref, gcg_ref, gmg_ref, misfit_ref,
    rows_v, rows_hi, rows_lo, list_s, list_r, kmat, scol, srow, tcol, pick,
    outb, inb, inb2, ser, xhat, rstd, sid, val_hi, val_lo,
    pool_m, pool_t, plen, gout_v, glow, mixed_v, xhat2, norm2, gnorm, rstd2,
    win_v, wout_v, gw, rc, ry, wx, rx, wz, rz, fin, gc, gtap_acc, small, rs1, rs2, rs3,
    ld_sem, idx_s, idx_r, row_s, row_r, back_s, back_r, halo_s, halo_r,
    core_s, core_r, y_s, y_r, x_s, x_r, z_s, z_r, s1_s, s1_r, s2_s, s2_r, s3_s, s3_r, f_s, f_r, *extra,
):
    if spare:
        ocol, orow, pick2, hop_a, hop_b, hop_c, hop_d, ret_a, ret_b, ret_c, ret_d = extra[:11]
        hop1_s, hop1_r, hop2_s, hop2_r, ret1_s, ret1_r, ret2_s, ret2_r = extra[11:]
    count, chans = rows_v.shape
    segs = mixed_v.shape[0]
    hidden = wout_v.shape[0]
    n_y, n_z = n_dp // 2, n_seq // NX
    group = 8
    n_groups = n_seq // group
    slots = group * cap
    dp, me = lax.axis_index("dp"), lax.axis_index("seq")
    y, core = lax.div(dp, 2), lax.rem(dp, 2)
    z, x = lax.div(me, NX), lax.rem(me, NX)
    my_group = lax.div(me, group)

    def remote(src, dst, send, recv, to_dp, to_seq):
        return pltpu.make_async_remote_copy(
            src_ref=src, dst_ref=dst, send_sem=send, recv_sem=recv,
            device_id=(to_dp, to_seq), device_id_type=MESH,
        )

    def each(n, fn, start=0):
        def step(i, carry):
            fn(i)
            return carry
        lax.fori_loop(start, n, step, 0)

    loads = [
        pltpu.make_async_copy(rows_hbm, rows_v, ld_sem.at[0]),
        pltpu.make_async_copy(win_hbm, win_v, ld_sem.at[1]),
        pltpu.make_async_copy(wout_hbm, wout_v, ld_sem.at[2]),
        pltpu.make_async_copy(gout_hbm, gout_v, ld_sem.at[3]),
    ]
    for load in loads:
        load.start()

    barrier = pltpu.get_barrier_semaphore()
    each(n_seq, lambda i: pl.semaphore_signal(
        barrier, inc=1, device_id=(dp, lax.rem(me + i, n_seq)), device_id_type=MESH), 1)
    each(n_dp, lambda i: pl.semaphore_signal(
        barrier, inc=1, device_id=(lax.rem(dp + i, n_dp), me), device_id_type=MESH), 1)

    order = order_ref[...]
    shift = count.bit_length() - 1
    owner = (order >> shift).astype(f32)
    local = order & (count - 1)
    local_hi = (local >> 5).astype(f32)
    local_lo = (local & 31).astype(f32)
    owner_col = jnp.transpose(jnp.broadcast_to(owner, (128, count)))
    lane = iota_f((128, 128), 1)
    below = ones_where(iota_f((128, 128), 0) > lane).astype(bf16)
    before = jnp.zeros((1, 128), f32)
    for b in range(count // 128):
        own_b = owner_col[b * 128:(b + 1) * 128]
        hot = ones_where(own_b == lane)
        ranks = mm(below, hot.astype(bf16)) + before
        before = before + jnp.sum(hot, axis=0, keepdims=True)
        rank = jnp.broadcast_to(jnp.sum(hot * ranks, axis=1, keepdims=True), (128, 128))
        slot = own_b * cap + rank
        if spare:
            via = rank + (me + 1 - cap).astype(f32)
            via = jnp.where(via >= n_seq, via - n_seq, via)
            ocol[b * 128:(b + 1) * 128, :] = jnp.where(rank >= cap, via, -1.0)
            slot = jnp.where(rank >= cap, -1.0, slot)
        scol[b * 128:(b + 1) * 128, :] = slot
        kmat[b * 128:(b + 1) * 128, :] = ones_where(rank == lane).astype(bf16)
    srow[...] = jnp.transpose(scol[...])[0:8, :]
    if spare:
        orow[...] = jnp.transpose(ocol[...])[0:8, :]
    owner_hot = ones_where(jnp.broadcast_to(owner, (n_seq, count)) == iota_f((n_seq, count), 0))
    kval = kmat[...]
    lists = (
        mm((owner_hot * local_hi).astype(bf16), kval) * 32.0
        + mm((owner_hot * local_lo).astype(bf16), kval)
        + mm(owner_hot.astype(bf16), kval)
        - 1.0
    )
    misfit = jnp.zeros((1, 1), f32)
    if spare:
        over = ones_where(before > cap)
        over_n = jnp.sum(jnp.maximum(before - cap, 0.0), axis=1, keepdims=True)
        over_from = jnp.sum(over * lane[0:1], axis=1, keepdims=True)
        misfit = misfit + ones_where(jnp.sum(over, axis=1, keepdims=True) > 1.0)
        place = iota_f((n_seq, 128), 0) - (me + 1).astype(f32)
        place = jnp.where(place < 0.0, place + n_seq, place)
        passed = jnp.where(place < over_n, over_from, -1.0)
        lists = jnp.where(iota_f((n_seq, 128), 1) == 64.0, passed, lists)
    for p in range(n_seq):
        list_s[p] = jnp.broadcast_to(lists[p:p + 1, :], (8, 128))
    list_r[me] = list_s[me]

    pl.semaphore_wait(barrier, n_seq - 1 + n_dp - 1)

    def send_list(i):
        p = lax.rem(me + i, n_seq)
        return remote(list_s.at[p], list_r.at[me], idx_s.at[p], idx_r.at[me], dp, p)

    def recv_list(i):
        p = lax.rem(me + i, n_seq)
        return remote(list_s.at[p], list_r.at[p], idx_s.at[p], idx_r.at[p], dp, p)

    each(n_seq, lambda i: send_list(i).start(), 1)

    loads[0].wait()

    def split_rows(i):
        at = pl.ds(pl.multiple_of(i * CH, CH), CH)
        rows_hi[at, :], rows_lo[at, :] = split_hi_lo(rows_v[at, :])

    each(count // CH, split_rows)
    each(n_seq, lambda i: recv_list(i).wait_recv(), 1)

    tcol[...] = jnp.transpose(list_r[...].reshape(n_seq * 8, 128))

    def hop_out(i, src, dst, send, recv):
        p = lax.rem(me + i, n_seq)
        return remote(src.at[p], dst.at[me], send.at[p], recv.at[me], dp, p)

    def hop_in(i, src, dst, send, recv):
        p = lax.rem(me + i, n_seq)
        return remote(src.at[p], dst.at[p], send.at[p], recv.at[p], dp, p)

    def hop_send(value, src, dst, send, recv):
        for p in range(n_seq):
            src[p] = value[p:p + 1, :]
        dst[me] = src[me]
        each(n_seq, lambda i: hop_out(i, src, dst, send, recv).start(), 1)

    def hop_read(src, dst, send, recv):
        each(n_seq, lambda i: hop_in(i, src, dst, send, recv).wait_recv(), 1)
        return split_hi_lo(jnp.concatenate([dst[p] for p in range(n_seq)], axis=0))

    if spare:
        flat = list_r[...].reshape(n_seq * 8, 128)
        wanted = jnp.max(flat, axis=0, keepdims=True)
        blocks = lax.broadcasted_iota(jnp.int32, (1, n_seq * 8), 1)
        busy = tcol[cap:cap + 1, :] >= 0.0
        over_to = jnp.max(jnp.where(busy, (blocks >> 3).astype(f32), -1.0), axis=1, keepdims=True)
        misfit = misfit + ones_where(jnp.sum(ones_where(busy), axis=1, keepdims=True) > 8.0)
        place = iota_f((n_seq, 128), 0) - 1.0 - over_to
        place = jnp.where(place < 0.0, place + n_seq, place)
        col = jnp.sum(jnp.where(iota_f((n_seq, 128), 1) == place + cap, wanted + 1.0, 0.0), axis=1, keepdims=True) - 1.0
        pick2[...] = ones_where(jnp.broadcast_to(col, (n_seq, count)) == iota_f((n_seq, count), 1)).astype(bf16)
        hop1 = (hop_a, hop_b, hop1_s, hop1_r)
        hop2 = (hop_c, hop_d, hop2_s, hop2_r)
        ret1 = (ret_a, ret_b, ret1_s, ret1_r)
        ret2 = (ret_c, ret_d, ret2_s, ret2_r)
        hop_send(mm(pick2[...], rows_hi[...]) + mm(pick2[...], rows_lo[...]), *hop1)
        rows_of = jnp.max(list_r[...], axis=1)
        passed_from = jnp.sum(
            jnp.where(iota_f((n_seq, 128), 1) == 64.0, rows_of, 0.0), axis=1, keepdims=True)
        pass_on = ones_where(
            jnp.broadcast_to(passed_from, (n_seq, n_seq)) == iota_f((n_seq, n_seq), 1)).astype(bf16)

    def row_out(p, src, dst, send, recv):
        return remote(src.at[p], dst.at[me], send.at[p], recv.at[me], dp, p)

    def row_self(src, dst, recv):
        return pltpu.make_async_copy(src.at[me], dst.at[me], recv.at[me])

    def launch(p0, dst, send, recv):
        def one(i):
            p = p0 + i

            @pl.when(p != me)
            def _():
                row_out(p, outb, dst, send, recv).start()

            @pl.when(p == me)
            def _():
                row_self(outb, dst, recv).start()
        each(group, one)

    def arrive(p0, dst, send, recv):
        def one(i):
            p = p0 + i

            @pl.when(p != me)
            def _():
                remote(outb.at[p], dst.at[p], send.at[p], recv.at[p], dp, p).wait_recv()

            @pl.when(p == me)
            def _():
                row_self(outb, dst, recv).wait()
        each(group, one)

    def group_out(g):
        return group * lax.rem(my_group + g, n_groups)

    def group_in(g):
        return group * lax.rem(my_group + n_groups - g, n_groups)

    tlane = lax.broadcasted_iota(jnp.int32, (cap, n_seq * 8), 1)
    rlane = iota_f((cap, count), 1)

    def gather_group(g):
        p0 = group_out(g)

        def one(i):
            p = p0 + i
            col = jnp.sum(jnp.where(tlane == p * 8, tcol[0:cap, :], 0.0), axis=1, keepdims=True)
            pick[pl.ds(pl.multiple_of(p * cap, 16), cap), :] = ones_where(
                jnp.broadcast_to(col, (cap, count)) == rlane).astype(bf16)
        each(group, one)
        hot = pick[pl.ds(pl.multiple_of(p0 * cap, 16), slots), :]
        made = mm(hot, rows_hi[...]) + mm(hot, rows_lo[...])
        outb[pl.ds(p0, group)] = made.reshape(group, cap, chans)
        launch(p0, inb, row_s, row_r)

    if spare:
        each(n_groups // 2, gather_group)
        high, low = hop_read(*hop1)
        hop_send(mm(pass_on, high) + mm(pass_on, low), *hop2)
        each(n_groups, gather_group, n_groups // 2)
    else:
        each(n_groups, gather_group)

    scene_n = scene_ref.shape[1]
    upto = ones_where(iota_f((scene_n, scene_n), 0) <= iota_f((scene_n, scene_n), 1))
    scene_ends = lax.dot_general(
        jnp.broadcast_to(scene_ref[...].astype(f32), (8, scene_n)), upto, (((1,), (0,)), ((), ())),
        precision=lax.Precision.HIGHEST, preferred_element_type=f32)[0:1, :]
    first_pos = (me * count - PAD).astype(f32)

    def scenes(i):
        start = pl.multiple_of(i * 8, 8)
        pos = iota_f((8, scene_n), 0) + (first_pos + start.astype(f32))
        ids = jnp.sum(ones_where(pos >= scene_ends), axis=1, keepdims=True)
        ids = jnp.where(pos[:, 0:1] < 0.0, -1.0, ids)
        sid[pl.ds(start, 8), :] = jnp.broadcast_to(ids, (8, 128))

    each(sid.shape[0] // 8, scenes)

    lens = jnp.broadcast_to(pool_ref[...].astype(f32), (128, segs))
    len_col = jnp.transpose(lens)
    plen[...] = len_col
    tri_rows, tri_cols = iota_f((segs, segs), 0), iota_f((segs, segs), 1)
    end_col = mm(ones_where(tri_cols <= tri_rows).astype(bf16), len_col.astype(bf16))
    end_row = mm(lens[0:8].astype(bf16), ones_where(tri_rows <= tri_cols).astype(bf16))[0:1, :]
    start_col = end_col - len_col
    start_row = end_row - lens[0:1]
    for t in range(count // 128):
        at_pos = iota_f((segs, 128), 1) + float(t * 128)
        pool_m[:, t * 128:(t + 1) * 128] = ones_where((at_pos >= start_col) & (at_pos < end_col)).astype(bf16)

    def pool_rows(i):
        start = pl.multiple_of(i * CH, CH)
        at_pos = iota_f((CH, segs), 0) + start.astype(f32)
        pool_t[pl.ds(start, CH), :] = ones_where((at_pos >= start_row) & (at_pos < end_row)).astype(bf16)

    each(count // CH, pool_rows)

    def clear(i):
        ser[pl.ds(pl.multiple_of(i * 8 + PAD, 8), 8), :] = jnp.zeros((8, chans), f32)

    each(count // 8, clear)
    gtap_acc[...] = jnp.zeros(gtap_acc.shape, f32)

    slane = iota_f((count, 128), 1)

    def place_group(g):
        p0 = group_in(g)
        arrive(p0, inb, row_s, row_r)
        high, low = split_hi_lo(inb[pl.ds(p0, group)].reshape(slots, chans))
        at_slot = scol[...] - (p0 * cap).astype(f32)
        hot = jnp.concatenate(
            [ones_where(at_slot == slane + float(128 * t)).astype(bf16) for t in range(slots // 128)], axis=1)
        ser[pl.ds(PAD, count), :] += mm(hot, high) + mm(hot, low)

    each(n_groups, place_group)
    if spare:
        high, low = hop_read(*hop2)
        hot = ones_where(ocol[:, 0:n_seq] == iota_f((count, n_seq), 1)).astype(bf16)
        ser[pl.ds(PAD, count), :] += mm(hot, high) + mm(hot, low)

    right, left = lax.rem(me + 1, n_seq), lax.rem(me + n_seq - 1, n_seq)

    def halo(buf, k):
        return (
            remote(buf.at[pl.ds(count, PAD)], buf.at[pl.ds(0, PAD)], halo_s.at[k], halo_r.at[k], dp, right),
            remote(buf.at[pl.ds(PAD, PAD)], buf.at[pl.ds(count + PAD, PAD)], halo_s.at[k + 1], halo_r.at[k + 1],
                   dp, left),
        )

    for copy in halo(ser, 0):
        copy.start()

    inv = 1.0 / chans

    def norm_rows(start, rows):
        at = pl.ds(start, rows)
        v = ser[at, :]
        centre = v - jnp.sum(v, axis=1, keepdims=True) * inv
        r = lax.rsqrt(jnp.sum(centre * centre, axis=1, keepdims=True) * inv + NORM_EPS)
        xhat[at, :] = centre * r
        rstd[at, :] = jnp.broadcast_to(r, (rows, 128))

    each(count // CH, lambda i: norm_rows(pl.multiple_of(i * CH + PAD, 8), CH))
    half = taps_ref.shape[0] // 2
    taps = taps_ref[...]
    cgain = cgain_ref[...]
    taps_gain = taps * cgain

    def conv_rows(i):
        base = pl.multiple_of(i * CH, CH)
        here = sid[pl.ds(base + PAD, CH), :]
        total = ser[pl.ds(base + PAD, CH), :]
        around = xhat[pl.ds(base, CH + 2 * PAD), :]
        for d in range(2 * half + 1):
            same = wide(ones_where(sid[pl.ds(base + PAD + d - half, CH), :] == here))
            total = total + taps_gain[d:d + 1, :] * (same * rows_from(around, PAD + d - half, CH))
        at = pl.ds(base, CH)
        val_hi[at, :], val_lo[at, :] = split_hi_lo(total)

    n_chunks = count // CH
    each(n_chunks - 1, conv_rows, 1)
    for copy in halo(ser, 0):
        copy.wait_recv()
    norm_rows(0, PAD)
    norm_rows(count + PAD, PAD)
    each(2, lambda i: conv_rows(i * (n_chunks - 1)))

    mixed_v[...] = mm(pool_m[...], val_hi[...]) + mm(pool_m[...], val_lo[...])
    mgain = mgain_ref[...]
    loads[3].wait()

    def norm_pooled(i):
        at = pl.ds(pl.multiple_of(i * CH, CH), CH)
        v = mixed_v[at, :] / wide(plen[at, :])
        centre = v - jnp.sum(v, axis=1, keepdims=True) * inv
        r = lax.rsqrt(jnp.sum(centre * centre, axis=1, keepdims=True) * inv + NORM_EPS)
        unit = centre * r
        mixed_v[at, :] = v
        xhat2[at, :] = unit
        norm2[at, :] = (unit * mgain).astype(bf16)
        rstd2[at, :] = jnp.broadcast_to(r, (CH, 128))
        glow[at, :] = gout_v[at, :].astype(bf16)
        gnorm[at, :] = jnp.zeros((CH, chans), f32)

    each(segs // CH, norm_pooled)
    loads[1].wait()
    loads[2].wait()

    hb = 512
    n_hb = hidden // hb
    n_cols = chans // 128
    partner = dp + 1 - 2 * core

    def core_copy(j):
        at = pl.ds(pl.multiple_of(j * hb, hb), hb)
        return remote(gw.at[1 - core, :, at, :], rc.at[:, at, :], core_s.at[j], core_r.at[j], partner, me)

    def mlp_block(j):
        at_h = pl.ds(pl.multiple_of(j * hb, hb), hb)
        w_in, w_out = win_v[:, at_h], wout_v[at_h, :]
        n2, gl = norm2[...], glow[...]
        rows_v[0:segs, :] = mm(n2, w_in)
        rows_v[segs:2 * segs, :] = mm_last(gl, w_out)

        def act(i):
            start = pl.multiple_of(i * 16, 16)
            at, at2 = pl.ds(start, 16), pl.ds(start + segs, 16)
            h, ga = rows_v[at, :], rows_v[at2, :]
            h2 = h * h
            t = jnp.tanh(h * (GELU_A + (GELU_A * GELU_B) * h2))
            half_t = 0.5 + 0.5 * t
            slope = half_t + (0.5 * h) * (1.0 - t * t) * (GELU_A + (3.0 * GELU_A * GELU_B) * h2)
            rows_hi[at, :] = (h * half_t).astype(bf16)
            rows_hi[at2, :] = (ga * slope).astype(bf16)

        each(segs // 16, act)
        active, gh = rows_hi[0:segs, :], rows_hi[segs:2 * segs, :]
        mixed_v[...] += mm(active, w_out)
        gnorm[...] += mm_last(gh, w_in)
        part_in, part_out = mm_first(gh, n2), mm_first(active, gl)
        for c in range(n_cols):
            gw[0, c, at_h, :] = part_in[:, c * 128:(c + 1) * 128]
            gw[1, c, at_h, :] = part_out[:, c * 128:(c + 1) * 128]
        core_copy(j).start()

    each(n_hb, mlp_block)
    store_mixed = pltpu.make_async_copy(mixed_v, mixed_hbm, ld_sem.at[4])
    store_mixed.start()

    small[...] = jnp.zeros(small.shape, f32)

    def norm_back(i):
        at = pl.ds(pl.multiple_of(i * CH, CH), CH)
        g, unit = gnorm[at, :], xhat2[at, :]
        prod = g * unit
        small[0:8, :] += fold8(prod)
        dx = g * mgain
        a = jnp.sum(dx, axis=1, keepdims=True) * inv
        b = jnp.sum(prod * mgain, axis=1, keepdims=True) * inv
        gp = gout_v[at, :] + wide(rstd2[at, :]) * (dx - a - unit * b)
        rows_hi[at, :], rows_lo[at, :] = split_hi_lo(gp / wide(plen[at, :]))

    each(segs // CH, norm_back)
    mgain_part = jnp.sum(small[0:8, :], axis=0, keepdims=True)
    gc[pl.ds(PAD, count), :] = mm(pool_t[...], rows_hi[0:segs, :]) + mm(pool_t[...], rows_lo[0:segs, :])
    for copy in halo(gc, 2):
        copy.start()

    per = 256
    n_per = hidden // per

    def add_core(i):
        c, k = lax.div(i, n_per), lax.rem(i, n_per)
        at = pl.ds(pl.multiple_of(k * per, per), per)
        gw[core, c, at, :] += rc[c, at, :]

    each(n_hb, lambda j: core_copy(j).wait_recv())
    each(n_cols * n_per, add_core)

    def y_send(o):
        yy = lax.rem(y + o, n_y)
        return remote(gw.at[core, yy], ry.at[o - 1], y_s.at[o - 1], y_r.at[o - 1], yy * 2 + core, me)

    each(n_y, lambda o: y_send(o).start(), 1)

    def back_rows(i):
        base = pl.multiple_of(i * CH, CH)
        own = pl.ds(base + PAD, CH)
        here, unit = sid[own, :], xhat[own, :]
        gl = jnp.zeros((CH, chans), f32)
        around = gc[pl.ds(base, CH + 2 * PAD), :]
        for e in range(-half, half + 1):
            same = wide(ones_where(sid[pl.ds(base + PAD + e, CH), :] == here)) * rows_from(around, PAD + e, CH)
            gl = gl + taps[half - e:half - e + 1, :] * same
            gtap_acc[half - e] += fold8(unit * same)
        dx = gl * cgain
        a = jnp.sum(dx, axis=1, keepdims=True) * inv
        b = jnp.sum(dx * unit, axis=1, keepdims=True) * inv
        gs = gc[own, :] + wide(rstd[own, :]) * (dx - a - unit * b)
        at = pl.ds(base, CH)
        val_hi[at, :], val_lo[at, :] = split_hi_lo(gs)

    each(n_chunks - 1, back_rows, 1)
    for copy in halo(gc, 2):
        copy.wait_recv()
    each(2, lambda i: back_rows(i * (n_chunks - 1)))

    def sent_all(i):
        p = lax.rem(me + i, n_seq)
        row_out(p, outb, inb, row_s, row_r).wait_send()

    each(n_seq, sent_all, 1)
    slot_at = iota_f((slots, count), 0)

    def return_group(g):
        p0 = group_out(g)
        hot = ones_where(slot_at == srow[0:1, :] - (p0 * cap).astype(f32)).astype(bf16)
        made = mm(hot, val_hi[...]) + mm(hot, val_lo[...])
        outb[pl.ds(p0, group)] = made.reshape(group, cap, chans)
        launch(p0, inb2, back_s, back_r)

    if spare:
        hot = ones_where(
            jnp.broadcast_to(orow[0:1, :], (n_seq, count)) == iota_f((n_seq, count), 0)).astype(bf16)
        hop_send(mm(hot, val_hi[...]) + mm(hot, val_lo[...]), *ret1)
        each(n_groups // 2, return_group)
        high, low = hop_read(*ret1)
        hop_send(mm_first(pass_on, high) + mm_first(pass_on, low), *ret2)
        each(n_groups, return_group, n_groups // 2)
    else:
        each(n_groups, return_group)

    for d in range(2 * half + 1):
        small[d:d + 1, :] = jnp.sum(gtap_acc[d], axis=0, keepdims=True)
    small[7:8, :] = mgain_part
    small[8:16, :] = jnp.broadcast_to(misfit, (8, chans))
    rs1[dp] = small[...]

    def s1_send(o):
        to = lax.rem(dp + o, n_dp)
        return remote(small, rs1.at[dp], s1_s.at[to], s1_r.at[dp], to, me)

    def s1_recv(o):
        to = lax.rem(dp + o, n_dp)
        return remote(small, rs1.at[to], s1_s.at[to], s1_r.at[to], to, me)

    each(n_dp, lambda o: s1_send(o).start(), 1)

    each(n_y, lambda o: y_send(o).wait_recv(), 1)

    def add_y(i):
        zz = lax.div(i, NX)
        xx = lax.rem(i, NX)
        at = pl.ds(pl.multiple_of(i * 64, 64), 64)
        total = gw[core, y, at, :]
        for o in range(n_y - 1):
            total = total + ry[o, at, :]
        wx[xx, zz] = total

    each(n_z * NX, add_y)
    each(n_dp, lambda o: s1_recv(o).wait_recv(), 1)
    total = rs1[0]
    for i in range(1, n_dp):
        total = total + rs1[i]
    rs2[x] = total

    def x_send(o):
        xx = lax.rem(x + o, NX)
        return remote(wx.at[xx], rx.at[o - 1], x_s.at[o - 1], x_r.at[o - 1], dp, z * NX + xx)

    def s2_send(o):
        xx = lax.rem(x + o, NX)
        return remote(rs2.at[x], rs2.at[x], s2_s.at[xx], s2_r.at[x], dp, z * NX + xx)

    def s2_recv(o):
        xx = lax.rem(x + o, NX)
        return remote(rs2.at[x], rs2.at[xx], s2_s.at[xx], s2_r.at[xx], dp, z * NX + xx)

    each(NX, lambda o: x_send(o).start(), 1)
    each(NX, lambda o: s2_send(o).start(), 1)
    each(NX, lambda o: x_send(o).wait_recv(), 1)

    def add_x(zz):
        total = wx[x, zz]
        for o in range(NX - 1):
            total = total + rx[o, zz]
        wz[zz] = total

    each(n_z, add_x)
    each(NX, lambda o: s2_recv(o).wait_recv(), 1)
    total = rs2[0]
    for i in range(1, NX):
        total = total + rs2[i]
    rs3[z] = total

    def z_send(o):
        zz = lax.rem(z + o, n_z)
        return remote(wz.at[zz], rz.at[o - 1], z_s.at[o - 1], z_r.at[o - 1], dp, zz * NX + x)

    def s3_send(o):
        zz = lax.rem(z + o, n_z)
        return remote(rs3.at[z], rs3.at[z], s3_s.at[zz], s3_r.at[z], dp, zz * NX + x)

    def s3_recv(o):
        zz = lax.rem(z + o, n_z)
        return remote(rs3.at[z], rs3.at[zz], s3_s.at[zz], s3_r.at[zz], dp, zz * NX + x)

    each(n_z, lambda o: z_send(o).start(), 1)
    each(n_z, lambda o: s3_send(o).start(), 1)
    each(n_z, lambda o: z_send(o).wait_recv(), 1)
    total = wz[z]
    for o in range(n_z - 1):
        total = total + rz[o]
    fin[core, y] = total

    def f_send(o):
        to = lax.rem(dp + o, n_dp)
        return remote(fin.at[core, y], fin.at[core, y], f_s.at[to], f_r.at[dp], to, me)

    def f_recv(o):
        to = lax.rem(dp + o, n_dp)
        part = fin.at[lax.rem(to, 2), lax.div(to, 2)]
        return remote(fin.at[core, y], part, f_s.at[to], f_r.at[to], to, me)

    each(n_dp, lambda o: f_send(o).start(), 1)
    each(n_z, lambda o: s3_recv(o).wait_recv(), 1)
    total = rs3[0]
    for i in range(1, n_z):
        total = total + rs3[i]
    gtaps_ref[...] = total[0:2 * half + 1, :] * cgain
    gcg_ref[...] = jnp.sum(total[0:2 * half + 1, :] * taps, axis=0, keepdims=True)
    gmg_ref[...] = total[7:8, :]
    misfit_ref[...] = total[8:16, 0:128]

    def clear_rows(i):
        rows_v[pl.ds(pl.multiple_of(i * 8, 8), 8), :] = jnp.zeros((8, chans), f32)

    each(count // 8, clear_rows)

    def settle_group(g):
        p0 = group_in(g)
        arrive(p0, inb2, back_s, back_r)
        high, low = split_hi_lo(inb2[pl.ds(p0, group)].reshape(slots, chans))
        hot = pick[pl.ds(pl.multiple_of(p0 * cap, 16), slots), :]
        rows_v[...] += mm_first(hot, high) + mm_first(hot, low)

    each(n_groups, settle_group)
    if spare:
        high, low = hop_read(*ret2)
        rows_v[...] += mm_first(pick2[...], high) + mm_first(pick2[...], low)
    store_rows = pltpu.make_async_copy(rows_v, grows_hbm, ld_sem.at[5])
    store_rows.start()

    each(n_dp, lambda o: f_recv(o).wait_recv(), 1)
    gwout_ref[...] = jnp.concatenate([fin[1, c] for c in range(n_cols)], axis=1)
    for c in range(n_cols):
        piece = jnp.concatenate([fin[0, c], jnp.zeros((64, 128), f32)], axis=0)
        gwin_ref[c * 128:(c + 1) * 128, :] = jnp.transpose(piece)[:, 0:64]

    each(n_seq, lambda i: send_list(i).wait_send(), 1)

    def back_sent(i):
        p = lax.rem(me + i, n_seq)
        row_out(p, outb, inb2, back_s, back_r).wait_send()

    each(n_seq, back_sent, 1)
    for copy in halo(ser, 0) + halo(gc, 2):
        copy.wait_send()
    each(n_hb, lambda j: core_copy(j).wait_send())
    each(n_y, lambda o: y_send(o).wait_send(), 1)
    each(NX, lambda o: x_send(o).wait_send(), 1)
    each(n_z, lambda o: z_send(o).wait_send(), 1)
    each(n_dp, lambda o: s1_send(o).wait_send(), 1)
    each(NX, lambda o: s2_send(o).wait_send(), 1)
    each(n_z, lambda o: s3_send(o).wait_send(), 1)
    each(n_dp, lambda o: f_send(o).wait_send(), 1)
    if spare:
        for hop in (hop1, hop2, ret1, ret2):
            each(n_seq, lambda i: hop_out(i, *hop).wait_send(), 1)
    store_mixed.wait()
    store_rows.wait()


def make_body(n_dp, n_seq):
    n_y, n_z = n_dp // 2, n_seq // NX

    def body(point_rows, serial_order, scene_counts, pool_counts, conv_gain, conv_kernel, mixer_gain,
             weight_in, weight_out, grad_out):
        count, chans = point_rows.shape
        segs = grad_out.shape[0]
        hidden = weight_out.shape[0]
        even = count // n_seq
        share = hidden // n_seq
        pads = count + 2 * PAD
        cols = chans // 128
        V = pltpu.VMEM
        D = lambda n: pltpu.SemaphoreType.DMA((n,))
        any_spec = pl.BlockSpec(memory_space=pl.ANY)
        vmem = pl.BlockSpec(memory_space=pltpu.VMEM)
        shape = jax.ShapeDtypeStruct
        scratch = lambda cap: [
            V((count, chans), f32), V((count, chans), bf16), V((count, chans), bf16),
            V((n_seq, 8, 128), f32), V((n_seq, 8, 128), f32), V((count, 128), bf16),
            V((count, 128), f32), V((8, count), f32), V((128, n_seq * 8), f32), V((n_seq * cap, count), bf16),
            V((n_seq, cap, chans), f32), V((n_seq, cap, chans), f32), V((n_seq, cap, chans), f32),
            V((pads, chans), f32), V((pads, chans), f32), V((pads, 128), f32), V((pads, 128), f32),
            V((count, chans), bf16), V((count, chans), bf16),
            V((segs, count), bf16), V((count, segs), bf16), V((segs, 128), f32),
            V((segs, chans), f32), V((segs, chans), bf16), V((segs, chans), f32), V((segs, chans), f32),
            V((segs, chans), bf16), V((segs, chans), f32), V((segs, 128), f32),
            V((chans, hidden), bf16), V((hidden, chans), bf16),
            V((2, cols, hidden, 128), f32), V((cols, hidden, 128), f32), V((n_y - 1, hidden, 128), f32),
            V((NX, n_z, share, 128), f32), V((NX - 1, n_z, share, 128), f32),
            V((n_z, share, 128), f32), V((n_z - 1, share, 128), f32), V((2, cols, share, 128), f32),
            V((pads, chans), f32), V((8, 8, chans), f32), V((16, chans), f32),
            V((n_dp, 16, chans), f32), V((NX, 16, chans), f32), V((n_z, 16, chans), f32),
            D(6), D(n_seq), D(n_seq), D(n_seq), D(n_seq), D(n_seq), D(n_seq), D(4), D(4),
            D(hidden // 512), D(hidden // 512), D(n_y), D(n_y), D(NX), D(NX), D(n_z), D(n_z),
            D(n_dp), D(n_dp), D(NX), D(NX), D(n_z), D(n_z), D(n_dp), D(n_dp),
        ]
        hop = [V((n_seq, 1, chans), f32)] * 8
        extra = [V((count, 128), f32), V((8, count), f32), V((n_seq, count), bf16)] + hop + [D(n_seq)] * 8

        def call(cap, spare, ident, name):
            return pl.pallas_call(
                lambda *refs: kernel(n_dp, n_seq, cap, spare, *refs),
                out_shape=(
                    shape((segs, chans), f32), shape((count, chans), f32), shape((chans, share), f32),
                    shape((share, chans), f32), shape(conv_kernel.shape, f32), shape((1, chans), f32),
                    shape((1, chans), f32), shape((8, 128), f32),
                ),
                in_specs=[any_spec] + [vmem] * 6 + [any_spec] * 3,
                out_specs=(any_spec, any_spec, vmem, vmem, vmem, vmem, vmem, vmem),
                scratch_shapes=scratch(cap) + (extra if spare else []),
                compiler_params=pltpu.CompilerParams(
                    collective_id=ident, has_side_effects=True, vmem_limit_bytes=62 * 1024 * 1024),
                name=name,
            )(
                point_rows, serial_order, scene_counts, pool_counts.reshape(1, segs), conv_gain[None], conv_kernel,
                mixer_gain[None], weight_in, weight_out, grad_out,
            )

        outs = call(even, even // 2, 0, "window_even")
        outs = lax.cond(
            outs[7][0, 0] > 0.0, lambda: call(even + even // 2, 0, 1, "window_full")[:7], lambda: outs[:7])
        mixed, grows, gwin, gwout, gtaps, gcg, gmg = outs
        return mixed, grows, gwin, gwout, gtaps, gcg[0], gmg[0]

    return body


def solution(mesh):
    return jax.shard_map(
        make_body(mesh.shape["dp"], mesh.shape["seq"]),
        mesh=mesh,
        in_specs=(
            P(("dp", "seq"), None), P("dp", "seq"), P("dp", None), P("dp", "seq", None), P(), P(), P(), P(), P(),
            P(("dp", "seq"), None),
        ),
        out_specs=(
            P(("dp", "seq"), None), P(("dp", "seq"), None), P(None, "seq"), P("seq", None), P(), P(), P(),
        ),
        check_vma=False,
    )
```

```python
import jax
import jax.numpy as jnp
from jax import lax
from jax.experimental import pallas as pl
from jax.experimental.pallas import tpu as pltpu
from jax.sharding import PartitionSpec as P

NORM_EPS = 1e-05
MESH = pl.DeviceIdType.MESH
f32, bf16 = jnp.float32, jnp.bfloat16
NX = 4
CH = 32
PAD = 8
GELU_A = 0.7978845608028654
GELU_B = 0.044715


def iota_f(shape, dim):
    return lax.broadcasted_iota(jnp.int32, shape, dim).astype(f32)


def ones_where(mask):
    return jnp.where(mask, 1.0, 0.0)


def split_hi_lo(value):
    high = value.astype(bf16)
    return high, (value - high.astype(f32)).astype(bf16)


def mm(a, b):
    return jnp.dot(a, b, preferred_element_type=f32)


def mm_last(a, b):
    return lax.dot_general(a, b, (((1,), (1,)), ((), ())), preferred_element_type=f32)


def mm_first(a, b):
    return lax.dot_general(a, b, (((0,), (0,)), ((), ())), preferred_element_type=f32)


def fold8(value):
    return jnp.sum(value.reshape(value.shape[0] // 8, 8, value.shape[1]), axis=0)


def rows_from(window, offset, count):
    size = window.shape[0]
    return pltpu.roll(window, (size - offset) % size, 0)[0:count]


def wide(value):
    return jnp.concatenate([value] * 4, axis=1)


def kernel(
    n_dp, n_seq, cap, spare,
    rows_hbm, order_ref, scene_ref, pool_ref, cgain_ref, taps_ref, mgain_ref, win_hbm, wout_hbm, gout_hbm,
    mixed_hbm, grows_hbm, gwin_ref, gwout_ref, gtaps_ref, gcg_ref, gmg_ref, misfit_ref,
    rows_v, rows_hl, list_s, list_r, kmat, scol, srow, tcol, pick,
    outb, inb, inb2, ser, xhat, rstd, sid, val_hl,
    pool_m, pool_t, plen, gout_v, glow, mixed_v, xhat2, norm2, gnorm, rstd2,
    win_v, wout_v, gw, rc, ry, wx, rx, wz, rz, fin, gc, gtap_acc, small, rs1, rs2, rs3,
    ld_sem, idx_s, idx_r, row_s, row_r, back_s, back_r, halo_s, halo_r,
    core_s, core_r, y_s, y_r, x_s, x_r, z_s, z_r, s1_s, s1_r, s2_s, s2_r, s3_s, s3_r, f_s, f_r, *extra,
):
    if spare:
        ocol, orow, pick2, hop_a, hop_b, hop_c, hop_d, ret_a, ret_b, ret_c, ret_d = extra[:11]
        hop1_s, hop1_r, hop2_s, hop2_r, ret1_s, ret1_r, ret2_s, ret2_r = extra[11:]
    count, chans = rows_v.shape
    segs = mixed_v.shape[0]
    rows_hi, rows_lo = rows_hl.at[pl.ds(0, count)], rows_hl.at[pl.ds(count, count)]
    val_hi, val_lo = val_hl.at[pl.ds(0, count)], val_hl.at[pl.ds(count, count)]
    hidden = wout_v.shape[0]
    n_y, n_z = n_dp // 2, n_seq // NX
    group = 8
    n_groups = n_seq // group
    slots = group * cap
    dp, me = lax.axis_index("dp"), lax.axis_index("seq")
    y, core = lax.div(dp, 2), lax.rem(dp, 2)
    z, x = lax.div(me, NX), lax.rem(me, NX)
    my_group = lax.div(me, group)

    def remote(src, dst, send, recv, to_dp, to_seq):
        return pltpu.make_async_remote_copy(
            src_ref=src, dst_ref=dst, send_sem=send, recv_sem=recv,
            device_id=(to_dp, to_seq), device_id_type=MESH,
        )

    def each(n, fn, start=0):
        def step(i, carry):
            fn(i)
            return carry
        lax.fori_loop(start, n, step, 0)

    loads = [
        pltpu.make_async_copy(rows_hbm, rows_v, ld_sem.at[0]),
        pltpu.make_async_copy(win_hbm, win_v, ld_sem.at[1]),
        pltpu.make_async_copy(wout_hbm, wout_v, ld_sem.at[2]),
        pltpu.make_async_copy(gout_hbm, gout_v, ld_sem.at[3]),
    ]
    for load in loads:
        load.start()

    barrier = pltpu.get_barrier_semaphore()
    each(n_seq, lambda i: pl.semaphore_signal(
        barrier, inc=1, device_id=(dp, lax.rem(me + i, n_seq)), device_id_type=MESH), 1)
    each(n_dp, lambda i: pl.semaphore_signal(
        barrier, inc=1, device_id=(lax.rem(dp + i, n_dp), me), device_id_type=MESH), 1)

    order = order_ref[...]
    shift = count.bit_length() - 1
    owner = (order >> shift).astype(f32)
    local = order & (count - 1)
    local_hi = (local >> 5).astype(f32)
    local_lo = (local & 31).astype(f32)
    owner_col = jnp.transpose(jnp.broadcast_to(owner, (128, count)))
    lane = iota_f((128, 128), 1)
    below = ones_where(iota_f((128, 128), 0) > lane).astype(bf16)
    before = jnp.zeros((1, 128), f32)
    for b in range(count // 128):
        own_b = owner_col[b * 128:(b + 1) * 128]
        hot = ones_where(own_b == lane)
        ranks = mm(below, hot.astype(bf16)) + before
        before = before + jnp.sum(hot, axis=0, keepdims=True)
        rank = jnp.broadcast_to(jnp.sum(hot * ranks, axis=1, keepdims=True), (128, 128))
        slot = own_b * cap + rank
        if spare:
            via = rank + (me + 1 - cap).astype(f32)
            via = jnp.where(via >= n_seq, via - n_seq, via)
            ocol[b * 128:(b + 1) * 128, :] = jnp.where(rank >= cap, via, -1.0)
            slot = jnp.where(rank >= cap, -1.0, slot)
        scol[b * 128:(b + 1) * 128, :] = slot
        kmat[b * 128:(b + 1) * 128, :] = ones_where(rank == lane).astype(bf16)
    srow[...] = jnp.transpose(scol[...])[0:8, :]
    if spare:
        orow[...] = jnp.transpose(ocol[...])[0:8, :]
    owner_hot = ones_where(jnp.broadcast_to(owner, (n_seq, count)) == iota_f((n_seq, count), 0))
    kval = kmat[...]
    lists = (
        mm((owner_hot * local_hi).astype(bf16), kval) * 32.0
        + mm((owner_hot * local_lo).astype(bf16), kval)
        + mm(owner_hot.astype(bf16), kval)
        - 1.0
    )
    misfit = jnp.zeros((1, 1), f32)
    if spare:
        over = ones_where(before > cap)
        over_n = jnp.sum(jnp.maximum(before - cap, 0.0), axis=1, keepdims=True)
        over_from = jnp.sum(over * lane[0:1], axis=1, keepdims=True)
        misfit = misfit + ones_where(jnp.sum(over, axis=1, keepdims=True) > 1.0)
        place = iota_f((n_seq, 128), 0) - (me + 1).astype(f32)
        place = jnp.where(place < 0.0, place + n_seq, place)
        passed = jnp.where(place < over_n, over_from, -1.0)
        lists = jnp.where(iota_f((n_seq, 128), 1) == 64.0, passed, lists)
    for p in range(n_seq):
        list_s[p] = jnp.broadcast_to(lists[p:p + 1, :], (8, 128))
    list_r[me] = list_s[me]

    pl.semaphore_wait(barrier, n_seq - 1 + n_dp - 1)

    def send_list(i):
        p = lax.rem(me + i, n_seq)
        return remote(list_s.at[p], list_r.at[me], idx_s.at[p], idx_r.at[me], dp, p)

    def recv_list(i):
        p = lax.rem(me + i, n_seq)
        return remote(list_s.at[p], list_r.at[p], idx_s.at[p], idx_r.at[p], dp, p)

    each(n_seq, lambda i: send_list(i).start(), 1)

    loads[0].wait()

    def split_rows(i):
        at = pl.ds(pl.multiple_of(i * CH, CH), CH)
        rows_hi[at, :], rows_lo[at, :] = split_hi_lo(rows_v[at, :])

    each(count // CH, split_rows)
    each(n_seq, lambda i: recv_list(i).wait_recv(), 1)

    tcol[...] = jnp.transpose(list_r[...].reshape(n_seq * 8, 128))

    def hop_out(i, src, dst, send, recv):
        p = lax.rem(me + i, n_seq)
        return remote(src.at[p], dst.at[me], send.at[p], recv.at[me], dp, p)

    def hop_in(i, src, dst, send, recv):
        p = lax.rem(me + i, n_seq)
        return remote(src.at[p], dst.at[p], send.at[p], recv.at[p], dp, p)

    def hop_send(value, src, dst, send, recv):
        for p in range(n_seq):
            src[p] = value[p:p + 1, :]
        dst[me] = src[me]
        each(n_seq, lambda i: hop_out(i, src, dst, send, recv).start(), 1)

    def hop_read(src, dst, send, recv):
        each(n_seq, lambda i: hop_in(i, src, dst, send, recv).wait_recv(), 1)
        return split_hi_lo(jnp.concatenate([dst[p] for p in range(n_seq)], axis=0))

    if spare:
        flat = list_r[...].reshape(n_seq * 8, 128)
        wanted = jnp.max(flat, axis=0, keepdims=True)
        blocks = lax.broadcasted_iota(jnp.int32, (1, n_seq * 8), 1)
        busy = tcol[cap:cap + 1, :] >= 0.0
        over_to = jnp.max(jnp.where(busy, (blocks >> 3).astype(f32), -1.0), axis=1, keepdims=True)
        misfit = misfit + ones_where(jnp.sum(ones_where(busy), axis=1, keepdims=True) > 8.0)
        place = iota_f((n_seq, 128), 0) - 1.0 - over_to
        place = jnp.where(place < 0.0, place + n_seq, place)
        col = jnp.sum(jnp.where(iota_f((n_seq, 128), 1) == place + cap, wanted + 1.0, 0.0), axis=1, keepdims=True) - 1.0
        pick2[...] = ones_where(jnp.broadcast_to(col, (n_seq, count)) == iota_f((n_seq, count), 1)).astype(bf16)
        hop1 = (hop_a, hop_b, hop1_s, hop1_r)
        hop2 = (hop_c, hop_d, hop2_s, hop2_r)
        ret1 = (ret_a, ret_b, ret1_s, ret1_r)
        ret2 = (ret_c, ret_d, ret2_s, ret2_r)
        hop_send(mm(pick2[...], rows_hi[...]) + mm(pick2[...], rows_lo[...]), *hop1)
        rows_of = jnp.max(list_r[...], axis=1)
        passed_from = jnp.sum(
            jnp.where(iota_f((n_seq, 128), 1) == 64.0, rows_of, 0.0), axis=1, keepdims=True)
        pass_on = ones_where(
            jnp.broadcast_to(passed_from, (n_seq, n_seq)) == iota_f((n_seq, n_seq), 1)).astype(bf16)

    def row_out(p, src, dst, send, recv):
        return remote(src.at[p], dst.at[me], send.at[p], recv.at[me], dp, p)

    def row_self(src, dst, recv):
        return pltpu.make_async_copy(src.at[me], dst.at[me], recv.at[me])

    def launch(p0, dst, send, recv):
        def one(i):
            p = p0 + i

            @pl.when(p != me)
            def _():
                row_out(p, outb, dst, send, recv).start()

            @pl.when(p == me)
            def _():
                row_self(outb, dst, recv).start()
        each(group, one)

    def arrive(p0, dst, send, recv):
        def one(i):
            p = p0 + i

            @pl.when(p != me)
            def _():
                remote(outb.at[p], dst.at[p], send.at[p], recv.at[p], dp, p).wait_recv()

            @pl.when(p == me)
            def _():
                row_self(outb, dst, recv).wait()
        each(group, one)

    def group_out(g):
        return group * lax.rem(my_group + g, n_groups)

    def group_in(g):
        return group * lax.rem(my_group + n_groups - g, n_groups)

    tlane = lax.broadcasted_iota(jnp.int32, (cap, n_seq * 8), 1)
    rlane = iota_f((cap, count), 1)

    def gather_group(g):
        p0 = group_out(g)

        def one(i):
            p = p0 + i
            col = jnp.sum(jnp.where(tlane == p * 8, tcol[0:cap, :], 0.0), axis=1, keepdims=True)
            pick[pl.ds(pl.multiple_of(p * cap, 16), cap), :] = ones_where(
                jnp.broadcast_to(col, (cap, count)) == rlane).astype(bf16)
        each(group, one)
        hot = pick[pl.ds(pl.multiple_of(p0 * cap, 16), slots), :]
        made = mm(hot, rows_hi[...]) + mm(hot, rows_lo[...])
        outb[pl.ds(p0, group)] = made.reshape(group, cap, chans)
        launch(p0, inb, row_s, row_r)

    if spare:
        each(n_groups // 2, gather_group)
        high, low = hop_read(*hop1)
        hop_send(mm(pass_on, high) + mm(pass_on, low), *hop2)
        each(n_groups, gather_group, n_groups // 2)
    else:
        each(n_groups, gather_group)

    scene_n = scene_ref.shape[1]
    upto = ones_where(iota_f((scene_n, scene_n), 0) <= iota_f((scene_n, scene_n), 1))
    scene_ends = lax.dot_general(
        jnp.broadcast_to(scene_ref[...].astype(f32), (8, scene_n)), upto, (((1,), (0,)), ((), ())),
        precision=lax.Precision.HIGHEST, preferred_element_type=f32)[0:1, :]
    first_pos = (me * count - PAD).astype(f32)

    def scenes(i):
        start = pl.multiple_of(i * 8, 8)
        pos = iota_f((8, scene_n), 0) + (first_pos + start.astype(f32))
        ids = jnp.sum(ones_where(pos >= scene_ends), axis=1, keepdims=True)
        ids = jnp.where(pos[:, 0:1] < 0.0, -1.0, ids)
        sid[pl.ds(start, 8), :] = jnp.broadcast_to(ids, (8, 128))

    each(sid.shape[0] // 8, scenes)

    lens = jnp.broadcast_to(pool_ref[...].astype(f32), (128, segs))
    len_col = jnp.transpose(lens)
    plen[...] = len_col
    tri_rows, tri_cols = iota_f((segs, segs), 0), iota_f((segs, segs), 1)
    end_col = mm(ones_where(tri_cols <= tri_rows).astype(bf16), len_col.astype(bf16))
    end_row = mm(lens[0:8].astype(bf16), ones_where(tri_rows <= tri_cols).astype(bf16))[0:1, :]
    start_col = end_col - len_col
    start_row = end_row - lens[0:1]
    for t in range(count // 128):
        at_pos = iota_f((segs, 128), 1) + float(t * 128)
        pool_m[:, t * 128:(t + 1) * 128] = ones_where((at_pos >= start_col) & (at_pos < end_col)).astype(bf16)

    def pool_rows(i):
        start = pl.multiple_of(i * CH, CH)
        at_pos = iota_f((CH, segs), 0) + start.astype(f32)
        pool_t[pl.ds(start, CH), :] = ones_where((at_pos >= start_row) & (at_pos < end_row)).astype(bf16)

    each(count // CH, pool_rows)

    def clear(i):
        ser[pl.ds(pl.multiple_of(i * 8 + PAD, 8), 8), :] = jnp.zeros((8, chans), f32)

    each(count // 8, clear)
    gtap_acc[...] = jnp.zeros(gtap_acc.shape, f32)

    slane = iota_f((count, 128), 1)

    def place_group(g):
        p0 = group_in(g)
        arrive(p0, inb, row_s, row_r)
        high, low = split_hi_lo(inb[pl.ds(p0, group)].reshape(slots, chans))
        at_slot = scol[...] - (p0 * cap).astype(f32)
        hot = jnp.concatenate(
            [ones_where(at_slot == slane + float(128 * t)).astype(bf16) for t in range(slots // 128)], axis=1)
        ser[pl.ds(PAD, count), :] += mm(hot, high) + mm(hot, low)

    each(n_groups, place_group)
    if spare:
        high, low = hop_read(*hop2)
        hot = ones_where(ocol[:, 0:n_seq] == iota_f((count, n_seq), 1)).astype(bf16)
        ser[pl.ds(PAD, count), :] += mm(hot, high) + mm(hot, low)

    right, left = lax.rem(me + 1, n_seq), lax.rem(me + n_seq - 1, n_seq)

    def halo(buf, k):
        return (
            remote(buf.at[pl.ds(count, PAD)], buf.at[pl.ds(0, PAD)], halo_s.at[k], halo_r.at[k], dp, right),
            remote(buf.at[pl.ds(PAD, PAD)], buf.at[pl.ds(count + PAD, PAD)], halo_s.at[k + 1], halo_r.at[k + 1],
                   dp, left),
        )

    for copy in halo(ser, 0):
        copy.start()

    inv = 1.0 / chans

    def norm_rows(start, rows):
        at = pl.ds(start, rows)
        v = ser[at, :]
        centre = v - jnp.sum(v, axis=1, keepdims=True) * inv
        r = lax.rsqrt(jnp.sum(centre * centre, axis=1, keepdims=True) * inv + NORM_EPS)
        xhat[at, :] = centre * r
        rstd[at, :] = jnp.broadcast_to(r, (rows, 128))

    each(count // CH, lambda i: norm_rows(pl.multiple_of(i * CH + PAD, 8), CH))
    half = taps_ref.shape[0] // 2
    taps = taps_ref[...]
    cgain = cgain_ref[...]
    taps_gain = taps * cgain

    def conv_rows(i):
        base = pl.multiple_of(i * CH, CH)
        here = sid[pl.ds(base + PAD, CH), :]
        total = ser[pl.ds(base + PAD, CH), :]
        around = xhat[pl.ds(base, CH + 2 * PAD), :]
        for d in range(2 * half + 1):
            same = wide(ones_where(sid[pl.ds(base + PAD + d - half, CH), :] == here))
            total = total + taps_gain[d:d + 1, :] * (same * rows_from(around, PAD + d - half, CH))
        at = pl.ds(base, CH)
        val_hi[at, :], val_lo[at, :] = split_hi_lo(total)

    n_chunks = count // CH
    each(n_chunks - 1, conv_rows, 1)
    for copy in halo(ser, 0):
        copy.wait_recv()
    norm_rows(0, PAD)
    norm_rows(count + PAD, PAD)
    each(2, lambda i: conv_rows(i * (n_chunks - 1)))

    mixed_v[...] = mm(pool_m[...], val_hi[...]) + mm(pool_m[...], val_lo[...])
    mgain = mgain_ref[...]
    loads[3].wait()

    def norm_pooled(i):
        at = pl.ds(pl.multiple_of(i * CH, CH), CH)
        v = mixed_v[at, :] / wide(plen[at, :])
        centre = v - jnp.sum(v, axis=1, keepdims=True) * inv
        r = lax.rsqrt(jnp.sum(centre * centre, axis=1, keepdims=True) * inv + NORM_EPS)
        unit = centre * r
        mixed_v[at, :] = v
        xhat2[at, :] = unit
        norm2[at, :] = (unit * mgain).astype(bf16)
        rstd2[at, :] = jnp.broadcast_to(r, (CH, 128))
        glow[at, :] = gout_v[at, :].astype(bf16)

    each(segs // CH, norm_pooled)
    loads[1].wait()
    loads[2].wait()

    hb = 512
    n_hb = hidden // hb
    n_cols = chans // 128
    partner = dp + 1 - 2 * core

    def core_copy(j):
        at = pl.ds(pl.multiple_of(j * hb, hb), hb)
        return remote(gw.at[1 - core, :, at, :], rc.at[:, at, :], core_s.at[j], core_r.at[j], partner, me)

    def mlp_block(j):
        at_h = pl.ds(pl.multiple_of(j * hb, hb), hb)
        w_in, w_out = win_v[:, at_h], wout_v[at_h, :]
        n2, gl = norm2[...], glow[...]
        rows_v[0:segs, :] = mm(n2, w_in)
        rows_v[segs:2 * segs, :] = mm_last(gl, w_out)

        def act(i):
            start = pl.multiple_of(i * 16, 16)
            at, at2 = pl.ds(start, 16), pl.ds(start + segs, 16)
            h, ga = rows_v[at, :], rows_v[at2, :]
            h2 = h * h
            t = jnp.tanh(h * (GELU_A + (GELU_A * GELU_B) * h2))
            half_t = 0.5 + 0.5 * t
            slope = half_t + (0.5 * h) * (1.0 - t * t) * (GELU_A + (3.0 * GELU_A * GELU_B) * h2)
            at_b = pl.ds(pl.multiple_of(start + j * segs, 16), 16)
            rows_hl[at_b, :] = (h * half_t).astype(bf16)
            val_hl[at_b, :] = (ga * slope).astype(bf16)

        each(segs // 16, act)
        at_j = pl.ds(pl.multiple_of(j * segs, segs), segs)
        part_in, part_out = mm_first(val_hl[at_j, :], n2), mm_first(rows_hl[at_j, :], gl)
        for c in range(n_cols):
            gw[0, c, at_h, :] = part_in[:, c * 128:(c + 1) * 128]
            gw[1, c, at_h, :] = part_out[:, c * 128:(c + 1) * 128]
        core_copy(j).start()

    per = 256
    n_per = hb // per

    def y_send(j, o):
        yy = lax.rem(y + o, n_y)
        at = pl.ds(pl.multiple_of(j * hb, hb), hb)
        k = j * n_y + o - 1
        return remote(gw.at[core, yy, at, :], ry.at[o - 1, at, :], y_s.at[k], y_r.at[k], yy * 2 + core, me)

    def core_done(j):
        core_copy(j).wait_recv()

        def add_core(i):
            c, k = lax.div(i, n_per), lax.rem(i, n_per)
            at = pl.ds(pl.multiple_of(j * hb + k * per, per), per)
            gw[core, c, at, :] += rc[c, at, :]

        each(n_cols * n_per, add_core)
        each(n_y, lambda o: y_send(j, o).start(), 1)

    def mlp_step(j):
        mlp_block(j)

        @pl.when(j > 0)
        def _():
            core_done(j - 1)

    each(n_hb, mlp_step)
    gnorm[...] = sum(
        mm_last(val_hl[j * segs:(j + 1) * segs, :], win_v[:, j * hb:(j + 1) * hb]) for j in range(n_hb))

    small[...] = jnp.zeros(small.shape, f32)

    def norm_back(i):
        at = pl.ds(pl.multiple_of(i * CH, CH), CH)
        g, unit = gnorm[at, :], xhat2[at, :]
        prod = g * unit
        small[0:8, :] += fold8(prod)
        dx = g * mgain
        a = jnp.sum(dx, axis=1, keepdims=True) * inv
        b = jnp.sum(prod * mgain, axis=1, keepdims=True) * inv
        gp = gout_v[at, :] + wide(rstd2[at, :]) * (dx - a - unit * b)
        val_hi[at, :], val_lo[at, :] = split_hi_lo(gp / wide(plen[at, :]))

    each(segs // CH, norm_back)
    mgain_part = jnp.sum(small[0:8, :], axis=0, keepdims=True)
    gc[pl.ds(PAD, count), :] = mm(pool_t[...], val_hi[0:segs, :]) + mm(pool_t[...], val_lo[0:segs, :])
    for copy in halo(gc, 2):
        copy.start()

    core_done(n_hb - 1)

    def back_rows(i):
        base = pl.multiple_of(i * CH, CH)
        own = pl.ds(base + PAD, CH)
        here, unit = sid[own, :], xhat[own, :]
        gl = jnp.zeros((CH, chans), f32)
        around = gc[pl.ds(base, CH + 2 * PAD), :]
        for e in range(-half, half + 1):
            same = wide(ones_where(sid[pl.ds(base + PAD + e, CH), :] == here)) * rows_from(around, PAD + e, CH)
            gl = gl + taps[half - e:half - e + 1, :] * same
            gtap_acc[half - e] += fold8(unit * same)
        dx = gl * cgain
        a = jnp.sum(dx, axis=1, keepdims=True) * inv
        b = jnp.sum(dx * unit, axis=1, keepdims=True) * inv
        gs = gc[own, :] + wide(rstd[own, :]) * (dx - a - unit * b)
        at = pl.ds(base, CH)
        val_hi[at, :], val_lo[at, :] = split_hi_lo(gs)

    each(n_chunks - 1, back_rows, 1)
    for copy in halo(gc, 2):
        copy.wait_recv()
    each(2, lambda i: back_rows(i * (n_chunks - 1)))

    def sent_all(i):
        p = lax.rem(me + i, n_seq)
        row_out(p, outb, inb, row_s, row_r).wait_send()

    each(n_seq, sent_all, 1)
    slot_at = iota_f((slots, count), 0)

    def return_group(g):
        p0 = group_out(g)
        hot = ones_where(slot_at == srow[0:1, :] - (p0 * cap).astype(f32)).astype(bf16)
        made = mm(hot, val_hi[...]) + mm(hot, val_lo[...])
        outb[pl.ds(p0, group)] = made.reshape(group, cap, chans)
        launch(p0, inb2, back_s, back_r)

    if spare:
        hot = ones_where(
            jnp.broadcast_to(orow[0:1, :], (n_seq, count)) == iota_f((n_seq, count), 0)).astype(bf16)
        hop_send(mm(hot, val_hi[...]) + mm(hot, val_lo[...]), *ret1)
        each(n_groups // 2, return_group)
        high, low = hop_read(*ret1)
        hop_send(mm_first(pass_on, high) + mm_first(pass_on, low), *ret2)
        each(n_groups, return_group, n_groups // 2)
    else:
        each(n_groups, return_group)

    for d in range(2 * half + 1):
        small[d:d + 1, :] = jnp.sum(gtap_acc[d], axis=0, keepdims=True)
    small[7:8, :] = mgain_part
    small[8:16, :] = jnp.broadcast_to(misfit, (8, chans))
    rs1[dp] = small[...]

    def s1_send(o):
        to = lax.rem(dp + o, n_dp)
        return remote(small, rs1.at[dp], s1_s.at[to], s1_r.at[dp], to, me)

    def s1_recv(o):
        to = lax.rem(dp + o, n_dp)
        return remote(small, rs1.at[to], s1_s.at[to], s1_r.at[to], to, me)

    each(n_dp, lambda o: s1_send(o).start(), 1)

    mixed_v[...] += sum(
        mm(rows_hl[j * segs:(j + 1) * segs, :], wout_v[j * hb:(j + 1) * hb, :]) for j in range(n_hb))
    store_mixed = pltpu.make_async_copy(mixed_v, mixed_hbm, ld_sem.at[4])
    store_mixed.start()

    share = hidden // n_seq
    z_per = n_z // n_hb

    def x_send(j, o):
        xx = lax.rem(x + o, NX)
        at, k = pl.ds(j * z_per, z_per), j * NX + o - 1
        return remote(wx.at[xx, at], rx.at[o - 1, at], x_s.at[k], x_r.at[k], dp, z * NX + xx)

    def y_done(j):
        each(n_y, lambda o: y_send(j, o).wait_recv(), 1)

        def add_y(i):
            zz, xx = j * z_per + lax.div(i, NX), lax.rem(i, NX)
            at = pl.ds(pl.multiple_of((zz * NX + xx) * share, share), share)
            total = gw[core, y, at, :]
            for o in range(n_y - 1):
                total = total + ry[o, at, :]
            wx[xx, zz] = total

        each(z_per * NX, add_y)
        each(NX, lambda o: x_send(j, o).start(), 1)

    each(n_hb, y_done)
    each(n_dp, lambda o: s1_recv(o).wait_recv(), 1)
    total = rs1[0]
    for i in range(1, n_dp):
        total = total + rs1[i]
    rs2[x] = total

    def s2_send(o):
        xx = lax.rem(x + o, NX)
        return remote(rs2.at[x], rs2.at[x], s2_s.at[xx], s2_r.at[x], dp, z * NX + xx)

    def s2_recv(o):
        xx = lax.rem(x + o, NX)
        return remote(rs2.at[x], rs2.at[xx], s2_s.at[xx], s2_r.at[xx], dp, z * NX + xx)

    each(NX, lambda o: s2_send(o).start(), 1)
    each(n_hb, lambda j: each(NX, lambda o: x_send(j, o).wait_recv(), 1))

    def add_x(zz):
        total = wx[x, zz]
        for o in range(NX - 1):
            total = total + rx[o, zz]
        wz[zz] = total

    each(n_z, add_x)
    each(NX, lambda o: s2_recv(o).wait_recv(), 1)
    total = rs2[0]
    for i in range(1, NX):
        total = total + rs2[i]
    rs3[z] = total

    def z_send(o):
        zz = lax.rem(z + o, n_z)
        return remote(wz.at[zz], rz.at[o - 1], z_s.at[o - 1], z_r.at[o - 1], dp, zz * NX + x)

    def s3_send(o):
        zz = lax.rem(z + o, n_z)
        return remote(rs3.at[z], rs3.at[z], s3_s.at[zz], s3_r.at[z], dp, zz * NX + x)

    def s3_recv(o):
        zz = lax.rem(z + o, n_z)
        return remote(rs3.at[z], rs3.at[zz], s3_s.at[zz], s3_r.at[zz], dp, zz * NX + x)

    each(n_z, lambda o: z_send(o).start(), 1)
    each(n_z, lambda o: s3_send(o).start(), 1)
    each(n_z, lambda o: z_send(o).wait_recv(), 1)
    total = wz[z]
    for o in range(n_z - 1):
        total = total + rz[o]
    fin[core, y] = total

    def f_send(o):
        to = lax.rem(dp + o, n_dp)
        return remote(fin.at[core, y], fin.at[core, y], f_s.at[to], f_r.at[dp], to, me)

    def f_recv(o):
        to = lax.rem(dp + o, n_dp)
        part = fin.at[lax.rem(to, 2), lax.div(to, 2)]
        return remote(fin.at[core, y], part, f_s.at[to], f_r.at[to], to, me)

    each(n_dp, lambda o: f_send(o).start(), 1)
    each(n_z, lambda o: s3_recv(o).wait_recv(), 1)
    total = rs3[0]
    for i in range(1, n_z):
        total = total + rs3[i]
    gtaps_ref[...] = total[0:2 * half + 1, :] * cgain
    gcg_ref[...] = jnp.sum(total[0:2 * half + 1, :] * taps, axis=0, keepdims=True)
    gmg_ref[...] = total[7:8, :]
    misfit_ref[...] = total[8:16, 0:128]

    def clear_rows(i):
        rows_v[pl.ds(pl.multiple_of(i * 8, 8), 8), :] = jnp.zeros((8, chans), f32)

    each(count // 8, clear_rows)

    def settle_group(g):
        p0 = group_in(g)
        arrive(p0, inb2, back_s, back_r)
        high, low = split_hi_lo(inb2[pl.ds(p0, group)].reshape(slots, chans))
        hot = pick[pl.ds(pl.multiple_of(p0 * cap, 16), slots), :]
        rows_v[...] += mm_first(hot, high) + mm_first(hot, low)

    each(n_groups, settle_group)
    if spare:
        high, low = hop_read(*ret2)
        rows_v[...] += mm_first(pick2[...], high) + mm_first(pick2[...], low)
    store_rows = pltpu.make_async_copy(rows_v, grows_hbm, ld_sem.at[5])
    store_rows.start()

    each(n_dp, lambda o: f_recv(o).wait_recv(), 1)
    gwout_ref[...] = jnp.concatenate([fin[1, c] for c in range(n_cols)], axis=1)
    for c in range(n_cols):
        piece = jnp.concatenate([fin[0, c], jnp.zeros((64, 128), f32)], axis=0)
        gwin_ref[c * 128:(c + 1) * 128, :] = jnp.transpose(piece)[:, 0:64]

    each(n_seq, lambda i: send_list(i).wait_send(), 1)

    def back_sent(i):
        p = lax.rem(me + i, n_seq)
        row_out(p, outb, inb2, back_s, back_r).wait_send()

    each(n_seq, back_sent, 1)
    for copy in halo(ser, 0) + halo(gc, 2):
        copy.wait_send()
    each(n_hb, lambda j: core_copy(j).wait_send())
    each(n_hb, lambda j: each(n_y, lambda o: y_send(j, o).wait_send(), 1))
    each(n_hb, lambda j: each(NX, lambda o: x_send(j, o).wait_send(), 1))
    each(n_z, lambda o: z_send(o).wait_send(), 1)
    each(n_dp, lambda o: s1_send(o).wait_send(), 1)
    each(NX, lambda o: s2_send(o).wait_send(), 1)
    each(n_z, lambda o: s3_send(o).wait_send(), 1)
    each(n_dp, lambda o: f_send(o).wait_send(), 1)
    if spare:
        for hop in (hop1, hop2, ret1, ret2):
            each(n_seq, lambda i: hop_out(i, *hop).wait_send(), 1)
    store_mixed.wait()
    store_rows.wait()


def make_body(n_dp, n_seq):
    n_y, n_z = n_dp // 2, n_seq // NX

    def body(point_rows, serial_order, scene_counts, pool_counts, conv_gain, conv_kernel, mixer_gain,
             weight_in, weight_out, grad_out):
        count, chans = point_rows.shape
        segs = grad_out.shape[0]
        hidden = weight_out.shape[0]
        even = count // n_seq
        share = hidden // n_seq
        pads = count + 2 * PAD
        cols = chans // 128
        V = pltpu.VMEM
        D = lambda n: pltpu.SemaphoreType.DMA((n,))
        any_spec = pl.BlockSpec(memory_space=pl.ANY)
        vmem = pl.BlockSpec(memory_space=pltpu.VMEM)
        shape = jax.ShapeDtypeStruct
        scratch = lambda cap: [
            V((count, chans), f32), V((2 * count, chans), bf16),
            V((n_seq, 8, 128), f32), V((n_seq, 8, 128), f32), V((count, 128), bf16),
            V((count, 128), f32), V((8, count), f32), V((128, n_seq * 8), f32), V((n_seq * cap, count), bf16),
            V((n_seq, cap, chans), f32), V((n_seq, cap, chans), f32), V((n_seq, cap, chans), f32),
            V((pads, chans), f32), V((pads, chans), f32), V((pads, 128), f32), V((pads, 128), f32),
            V((2 * count, chans), bf16),
            V((segs, count), bf16), V((count, segs), bf16), V((segs, 128), f32),
            V((segs, chans), f32), V((segs, chans), bf16), V((segs, chans), f32), V((segs, chans), f32),
            V((segs, chans), bf16), V((segs, chans), f32), V((segs, 128), f32),
            V((chans, hidden), bf16), V((hidden, chans), bf16),
            V((2, cols, hidden, 128), f32), V((cols, hidden, 128), f32), V((n_y - 1, hidden, 128), f32),
            V((NX, n_z, share, 128), f32), V((NX - 1, n_z, share, 128), f32),
            V((n_z, share, 128), f32), V((n_z - 1, share, 128), f32), V((2, cols, share, 128), f32),
            V((pads, chans), f32), V((8, 8, chans), f32), V((16, chans), f32),
            V((n_dp, 16, chans), f32), V((NX, 16, chans), f32), V((n_z, 16, chans), f32),
            D(6), D(n_seq), D(n_seq), D(n_seq), D(n_seq), D(n_seq), D(n_seq), D(4), D(4),
            D(hidden // 512), D(hidden // 512), D(4 * n_y), D(4 * n_y), D(4 * NX), D(4 * NX), D(n_z), D(n_z),
            D(n_dp), D(n_dp), D(NX), D(NX), D(n_z), D(n_z), D(n_dp), D(n_dp),
        ]
        hop = [V((n_seq, 1, chans), f32)] * 8
        extra = [V((count, 128), f32), V((8, count), f32), V((n_seq, count), bf16)] + hop + [D(n_seq)] * 8

        def call(cap, spare, ident, name):
            return pl.pallas_call(
                lambda *refs: kernel(n_dp, n_seq, cap, spare, *refs),
                out_shape=(
                    shape((segs, chans), f32), shape((count, chans), f32), shape((chans, share), f32),
                    shape((share, chans), f32), shape(conv_kernel.shape, f32), shape((1, chans), f32),
                    shape((1, chans), f32), shape((8, 128), f32),
                ),
                in_specs=[any_spec] + [vmem] * 6 + [any_spec] * 3,
                out_specs=(any_spec, any_spec, vmem, vmem, vmem, vmem, vmem, vmem),
                scratch_shapes=scratch(cap) + (extra if spare else []),
                compiler_params=pltpu.CompilerParams(
                    collective_id=ident, has_side_effects=True, vmem_limit_bytes=62 * 1024 * 1024),
                name=name,
            )(
                point_rows, serial_order, scene_counts, pool_counts.reshape(1, segs), conv_gain[None], conv_kernel,
                mixer_gain[None], weight_in, weight_out, grad_out,
            )

        outs = call(even, even // 2, 0, "window_even")
        outs = lax.cond(
            outs[7][0, 0] > 0.0, lambda: call(even + even // 2, 0, 1, "window_full")[:7], lambda: outs[:7])
        mixed, grows, gwin, gwout, gtaps, gcg, gmg = outs
        return mixed, grows, gwin, gwout, gtaps, gcg[0], gmg[0]

    return body


def solution(mesh):
    return jax.shard_map(
        make_body(mesh.shape["dp"], mesh.shape["seq"]),
        mesh=mesh,
        in_specs=(
            P(("dp", "seq"), None), P("dp", "seq"), P("dp", None), P("dp", "seq", None), P(), P(), P(), P(), P(),
            P(("dp", "seq"), None),
        ),
        out_specs=(
            P(("dp", "seq"), None), P(("dp", "seq"), None), P(None, "seq"), P("seq", None), P(), P(), P(),
        ),
        check_vma=False,
    )
```

```python
import jax
import jax.numpy as jnp
from jax import lax
from jax.experimental import pallas as pl
from jax.experimental.pallas import tpu as pltpu
from jax.sharding import PartitionSpec as P

NORM_EPS = 1e-05
MESH = pl.DeviceIdType.MESH
f32, bf16 = jnp.float32, jnp.bfloat16
NX = 4
CH = 32
NB = 128
CB = 64
PAD = 8
GELU_A = 0.7978845608028654
GELU_B = 0.044715


def iota_f(shape, dim):
    return lax.broadcasted_iota(jnp.int32, shape, dim).astype(f32)


def ones_where(mask):
    return jnp.where(mask, 1.0, 0.0)


def split_hi_lo(value):
    high = value.astype(bf16)
    return high, (value - high.astype(f32)).astype(bf16)


def mm(a, b):
    return jnp.dot(a, b, preferred_element_type=f32)


def mm_last(a, b):
    return lax.dot_general(a, b, (((1,), (1,)), ((), ())), preferred_element_type=f32)


def mm_first(a, b):
    return lax.dot_general(a, b, (((0,), (0,)), ((), ())), preferred_element_type=f32)


def fold8(value):
    return jnp.sum(value.reshape(value.shape[0] // 8, 8, value.shape[1]), axis=0)


def rows_from(window, offset, count):
    size = window.shape[0]
    return pltpu.roll(window, (size - offset) % size, 0)[0:count]


def wide(value):
    return jnp.concatenate([value] * 4, axis=1)


def kernel(
    n_dp, n_seq, cap, spare,
    rows_hbm, order_ref, scene_ref, pool_ref, cgain_ref, taps_ref, mgain_ref, win_hbm, wout_hbm, gout_hbm,
    mixed_hbm, grows_hbm, gwin_ref, gwout_ref, gtaps_ref, gcg_ref, gmg_ref, misfit_ref,
    rows_v, rows_hl, list_s, list_r, kmat, scol, srow, tcol, pick,
    outb, inb, inb2, ser, xhat, rstd, sid, val_hl,
    pool_m, pool_t, plen, gout_v, glow, mixed_v, xhat2, norm2, gnorm, rstd2,
    win_v, wout_v, gw, rc, ry, wx, rx, wz, rz, fin, gc, gtap_acc, small, rs1, rs2, rs3,
    ld_sem, idx_s, idx_r, row_s, row_r, back_s, back_r, halo_s, halo_r,
    core_s, core_r, y_s, y_r, x_s, x_r, z_s, z_r, s1_s, s1_r, s2_s, s2_r, s3_s, s3_r, f_s, f_r, *extra,
):
    if spare:
        ocol, orow, pick2, hop_a, hop_b, hop_c, hop_d, ret_a, ret_b, ret_c, ret_d = extra[:11]
        hop1_s, hop1_r, hop2_s, hop2_r, ret1_s, ret1_r, ret2_s, ret2_r = extra[11:]
    count, chans = rows_v.shape
    segs = mixed_v.shape[0]
    rows_hi, rows_lo = rows_hl.at[pl.ds(0, count)], rows_hl.at[pl.ds(count, count)]
    val_hi, val_lo = val_hl.at[pl.ds(0, count)], val_hl.at[pl.ds(count, count)]
    hidden = wout_v.shape[0]
    n_y, n_z = n_dp // 2, n_seq // NX
    group = 8
    n_groups = n_seq // group
    slots = group * cap
    dp, me = lax.axis_index("dp"), lax.axis_index("seq")
    y, core = lax.div(dp, 2), lax.rem(dp, 2)
    z, x = lax.div(me, NX), lax.rem(me, NX)
    my_group = lax.div(me, group)

    def remote(src, dst, send, recv, to_dp, to_seq):
        return pltpu.make_async_remote_copy(
            src_ref=src, dst_ref=dst, send_sem=send, recv_sem=recv,
            device_id=(to_dp, to_seq), device_id_type=MESH,
        )

    def each(n, fn, start=0):
        def step(i, carry):
            fn(i)
            return carry
        lax.fori_loop(start, n, step, 0)

    loads = [
        pltpu.make_async_copy(rows_hbm, rows_v, ld_sem.at[0]),
        pltpu.make_async_copy(win_hbm, win_v, ld_sem.at[1]),
        pltpu.make_async_copy(wout_hbm, wout_v, ld_sem.at[2]),
        pltpu.make_async_copy(gout_hbm, gout_v, ld_sem.at[3]),
    ]
    for load in loads:
        load.start()

    barrier = pltpu.get_barrier_semaphore()
    each(n_seq, lambda i: pl.semaphore_signal(
        barrier, inc=1, device_id=(dp, lax.rem(me + i, n_seq)), device_id_type=MESH), 1)
    each(n_dp, lambda i: pl.semaphore_signal(
        barrier, inc=1, device_id=(lax.rem(dp + i, n_dp), me), device_id_type=MESH), 1)

    order = order_ref[...]
    shift = count.bit_length() - 1
    owner = (order >> shift).astype(f32)
    local = order & (count - 1)
    local_hi = (local >> 5).astype(f32)
    local_lo = (local & 31).astype(f32)
    owner_col = jnp.transpose(jnp.broadcast_to(owner, (128, count)))
    lane = iota_f((128, 128), 1)
    below = ones_where(iota_f((128, 128), 0) > lane).astype(bf16)
    before = jnp.zeros((1, 128), f32)
    for b in range(count // 128):
        own_b = owner_col[b * 128:(b + 1) * 128]
        hot = ones_where(own_b == lane)
        ranks = mm(below, hot.astype(bf16)) + before
        before = before + jnp.sum(hot, axis=0, keepdims=True)
        rank = jnp.broadcast_to(jnp.sum(hot * ranks, axis=1, keepdims=True), (128, 128))
        slot = own_b * cap + rank
        if spare:
            via = rank + (me + 1 - cap).astype(f32)
            via = jnp.where(via >= n_seq, via - n_seq, via)
            ocol[b * 128:(b + 1) * 128, :] = jnp.where(rank >= cap, via, -1.0)
            slot = jnp.where(rank >= cap, -1.0, slot)
        scol[b * 128:(b + 1) * 128, :] = slot
        kmat[b * 128:(b + 1) * 128, :] = ones_where(rank == lane).astype(bf16)
    srow[...] = jnp.transpose(scol[...])[0:8, :]
    if spare:
        orow[...] = jnp.transpose(ocol[...])[0:8, :]
    owner_hot = ones_where(jnp.broadcast_to(owner, (n_seq, count)) == iota_f((n_seq, count), 0))
    kval = kmat[...]
    lists = (
        mm((owner_hot * local_hi).astype(bf16), kval) * 32.0
        + mm((owner_hot * local_lo).astype(bf16), kval)
        + mm(owner_hot.astype(bf16), kval)
        - 1.0
    )
    misfit = jnp.zeros((1, 1), f32)
    if spare:
        over = ones_where(before > cap)
        over_n = jnp.sum(jnp.maximum(before - cap, 0.0), axis=1, keepdims=True)
        over_from = jnp.sum(over * lane[0:1], axis=1, keepdims=True)
        misfit = misfit + ones_where(jnp.sum(over, axis=1, keepdims=True) > 1.0)
        place = iota_f((n_seq, 128), 0) - (me + 1).astype(f32)
        place = jnp.where(place < 0.0, place + n_seq, place)
        passed = jnp.where(place < over_n, over_from, -1.0)
        lists = jnp.where(iota_f((n_seq, 128), 1) == 64.0, passed, lists)
    for p in range(n_seq):
        list_s[p] = jnp.broadcast_to(lists[p:p + 1, :], (8, 128))
    list_r[me] = list_s[me]

    pl.semaphore_wait(barrier, n_seq - 1 + n_dp - 1)

    def send_list(i):
        p = lax.rem(me + i, n_seq)
        return remote(list_s.at[p], list_r.at[me], idx_s.at[p], idx_r.at[me], dp, p)

    def recv_list(i):
        p = lax.rem(me + i, n_seq)
        return remote(list_s.at[p], list_r.at[p], idx_s.at[p], idx_r.at[p], dp, p)

    each(n_seq, lambda i: send_list(i).start(), 1)

    loads[0].wait()

    def split_rows(i):
        at = pl.ds(pl.multiple_of(i * CH, CH), CH)
        rows_hi[at, :], rows_lo[at, :] = split_hi_lo(rows_v[at, :])

    each(count // CH, split_rows)
    each(n_seq, lambda i: recv_list(i).wait_recv(), 1)

    tcol[...] = jnp.transpose(list_r[...].reshape(n_seq * 8, 128))

    def hop_out(i, src, dst, send, recv):
        p = lax.rem(me + i, n_seq)
        return remote(src.at[p], dst.at[me], send.at[p], recv.at[me], dp, p)

    def hop_in(i, src, dst, send, recv):
        p = lax.rem(me + i, n_seq)
        return remote(src.at[p], dst.at[p], send.at[p], recv.at[p], dp, p)

    def hop_send(value, src, dst, send, recv):
        for p in range(n_seq):
            src[p] = value[p:p + 1, :]
        dst[me] = src[me]
        each(n_seq, lambda i: hop_out(i, src, dst, send, recv).start(), 1)

    def hop_read(src, dst, send, recv):
        each(n_seq, lambda i: hop_in(i, src, dst, send, recv).wait_recv(), 1)
        return split_hi_lo(jnp.concatenate([dst[p] for p in range(n_seq)], axis=0))

    if spare:
        flat = list_r[...].reshape(n_seq * 8, 128)
        wanted = jnp.max(flat, axis=0, keepdims=True)
        blocks = lax.broadcasted_iota(jnp.int32, (1, n_seq * 8), 1)
        busy = tcol[cap:cap + 1, :] >= 0.0
        over_to = jnp.max(jnp.where(busy, (blocks >> 3).astype(f32), -1.0), axis=1, keepdims=True)
        misfit = misfit + ones_where(jnp.sum(ones_where(busy), axis=1, keepdims=True) > 8.0)
        place = iota_f((n_seq, 128), 0) - 1.0 - over_to
        place = jnp.where(place < 0.0, place + n_seq, place)
        col = jnp.sum(jnp.where(iota_f((n_seq, 128), 1) == place + cap, wanted + 1.0, 0.0), axis=1, keepdims=True) - 1.0
        pick2[...] = ones_where(jnp.broadcast_to(col, (n_seq, count)) == iota_f((n_seq, count), 1)).astype(bf16)
        hop1 = (hop_a, hop_b, hop1_s, hop1_r)
        hop2 = (hop_c, hop_d, hop2_s, hop2_r)
        ret1 = (ret_a, ret_b, ret1_s, ret1_r)
        ret2 = (ret_c, ret_d, ret2_s, ret2_r)
        hop_send(mm(pick2[...], rows_hi[...]) + mm(pick2[...], rows_lo[...]), *hop1)
        rows_of = jnp.max(list_r[...], axis=1)
        passed_from = jnp.sum(
            jnp.where(iota_f((n_seq, 128), 1) == 64.0, rows_of, 0.0), axis=1, keepdims=True)
        pass_on = ones_where(
            jnp.broadcast_to(passed_from, (n_seq, n_seq)) == iota_f((n_seq, n_seq), 1)).astype(bf16)

    def row_out(p, src, dst, send, recv):
        return remote(src.at[p], dst.at[me], send.at[p], recv.at[me], dp, p)

    def row_self(src, dst, recv):
        return pltpu.make_async_copy(src.at[me], dst.at[me], recv.at[me])

    def launch(p0, dst, send, recv):
        def one(i):
            p = p0 + i

            @pl.when(p != me)
            def _():
                row_out(p, outb, dst, send, recv).start()

            @pl.when(p == me)
            def _():
                row_self(outb, dst, recv).start()
        each(group, one)

    def arrive(p0, dst, send, recv):
        def one(i):
            p = p0 + i

            @pl.when(p != me)
            def _():
                remote(outb.at[p], dst.at[p], send.at[p], recv.at[p], dp, p).wait_recv()

            @pl.when(p == me)
            def _():
                row_self(outb, dst, recv).wait()
        each(group, one)

    def group_out(g):
        return group * lax.rem(my_group + g, n_groups)

    def group_in(g):
        return group * lax.rem(my_group + n_groups - g, n_groups)

    tlane = lax.broadcasted_iota(jnp.int32, (cap, n_seq * 8), 1)
    rlane = iota_f((cap, count), 1)

    def gather_group(g):
        p0 = group_out(g)

        def one(i):
            p = p0 + i
            col = jnp.sum(jnp.where(tlane == p * 8, tcol[0:cap, :], 0.0), axis=1, keepdims=True)
            pick[pl.ds(pl.multiple_of(p * cap, 16), cap), :] = ones_where(
                jnp.broadcast_to(col, (cap, count)) == rlane).astype(bf16)
        each(group, one)
        hot = pick[pl.ds(pl.multiple_of(p0 * cap, 16), slots), :]
        made = mm(hot, rows_hi[...]) + mm(hot, rows_lo[...])
        outb[pl.ds(p0, group)] = made.reshape(group, cap, chans)
        launch(p0, inb, row_s, row_r)

    if spare:
        each(n_groups // 2, gather_group)
        high, low = hop_read(*hop1)
        hop_send(mm(pass_on, high) + mm(pass_on, low), *hop2)
        each(n_groups, gather_group, n_groups // 2)
    else:
        each(n_groups, gather_group)

    scene_n = scene_ref.shape[1]
    upto = ones_where(iota_f((scene_n, scene_n), 0) <= iota_f((scene_n, scene_n), 1))
    scene_ends = lax.dot_general(
        jnp.broadcast_to(scene_ref[...].astype(f32), (8, scene_n)), upto, (((1,), (0,)), ((), ())),
        precision=lax.Precision.HIGHEST, preferred_element_type=f32)[0:1, :]
    first_pos = (me * count - PAD).astype(f32)

    def scenes(i):
        start = pl.multiple_of(i * 8, 8)
        pos = iota_f((8, scene_n), 0) + (first_pos + start.astype(f32))
        ids = jnp.sum(ones_where(pos >= scene_ends), axis=1, keepdims=True)
        ids = jnp.where(pos[:, 0:1] < 0.0, -1.0, ids)
        sid[pl.ds(start, 8), :] = jnp.broadcast_to(ids, (8, 128))

    each(sid.shape[0] // 8, scenes)

    lens = jnp.broadcast_to(pool_ref[...].astype(f32), (128, segs))
    len_col = jnp.transpose(lens)
    plen[...] = len_col
    tri_rows, tri_cols = iota_f((segs, segs), 0), iota_f((segs, segs), 1)
    end_col = mm(ones_where(tri_cols <= tri_rows).astype(bf16), len_col.astype(bf16))
    end_row = mm(lens[0:8].astype(bf16), ones_where(tri_rows <= tri_cols).astype(bf16))[0:1, :]
    start_col = end_col - len_col
    start_row = end_row - lens[0:1]
    for t in range(count // 128):
        at_pos = iota_f((segs, 128), 1) + float(t * 128)
        pool_m[:, t * 128:(t + 1) * 128] = ones_where((at_pos >= start_col) & (at_pos < end_col)).astype(bf16)

    def pool_rows(i):
        start = pl.multiple_of(i * CH, CH)
        at_pos = iota_f((CH, segs), 0) + start.astype(f32)
        pool_t[pl.ds(start, CH), :] = ones_where((at_pos >= start_row) & (at_pos < end_row)).astype(bf16)

    each(count // CH, pool_rows)

    def clear(i):
        ser[pl.ds(pl.multiple_of(i * 8 + PAD, 8), 8), :] = jnp.zeros((8, chans), f32)

    each(count // 8, clear)
    gtap_acc[...] = jnp.zeros(gtap_acc.shape, f32)

    slane = iota_f((count, 128), 1)

    def place_group(g):
        p0 = group_in(g)
        arrive(p0, inb, row_s, row_r)
        high, low = split_hi_lo(inb[pl.ds(p0, group)].reshape(slots, chans))
        at_slot = scol[...] - (p0 * cap).astype(f32)
        hot = jnp.concatenate(
            [ones_where(at_slot == slane + float(128 * t)).astype(bf16) for t in range(slots // 128)], axis=1)
        ser[pl.ds(PAD, count), :] += mm(hot, high) + mm(hot, low)

    each(n_groups, place_group)
    if spare:
        high, low = hop_read(*hop2)
        hot = ones_where(ocol[:, 0:n_seq] == iota_f((count, n_seq), 1)).astype(bf16)
        ser[pl.ds(PAD, count), :] += mm(hot, high) + mm(hot, low)

    right, left = lax.rem(me + 1, n_seq), lax.rem(me + n_seq - 1, n_seq)

    def halo(buf, k):
        return (
            remote(buf.at[pl.ds(count, PAD)], buf.at[pl.ds(0, PAD)], halo_s.at[k], halo_r.at[k], dp, right),
            remote(buf.at[pl.ds(PAD, PAD)], buf.at[pl.ds(count + PAD, PAD)], halo_s.at[k + 1], halo_r.at[k + 1],
                   dp, left),
        )

    for copy in halo(ser, 0):
        copy.start()

    inv = 1.0 / chans

    def norm_rows(start, rows):
        at = pl.ds(start, rows)
        v = ser[at, :]
        centre = v - jnp.sum(v, axis=1, keepdims=True) * inv
        r = lax.rsqrt(jnp.sum(centre * centre, axis=1, keepdims=True) * inv + NORM_EPS)
        xhat[at, :] = centre * r
        rstd[at, :] = jnp.broadcast_to(r, (rows, 128))

    each(count // NB, lambda i: norm_rows(pl.multiple_of(i * NB + PAD, 8), NB))
    half = taps_ref.shape[0] // 2
    taps = taps_ref[...]
    cgain = cgain_ref[...]
    taps_gain = taps * cgain

    def conv_rows(i):
        base = pl.multiple_of(i * CH, CH)
        here = sid[pl.ds(base + PAD, CH), :]
        total = ser[pl.ds(base + PAD, CH), :]
        around = xhat[pl.ds(base, CH + 2 * PAD), :]
        for d in range(2 * half + 1):
            same = wide(ones_where(sid[pl.ds(base + PAD + d - half, CH), :] == here))
            total = total + taps_gain[d:d + 1, :] * (same * rows_from(around, PAD + d - half, CH))
        at = pl.ds(base, CH)
        val_hi[at, :], val_lo[at, :] = split_hi_lo(total)

    n_chunks = count // CH
    each(n_chunks - 1, conv_rows, 1)
    for copy in halo(ser, 0):
        copy.wait_recv()
    norm_rows(0, PAD)
    norm_rows(count + PAD, PAD)
    each(2, lambda i: conv_rows(i * (n_chunks - 1)))

    mixed_v[...] = mm(pool_m[...], val_hi[...]) + mm(pool_m[...], val_lo[...])
    mgain = mgain_ref[...]
    loads[3].wait()

    def norm_pooled(i):
        at = pl.ds(pl.multiple_of(i * NB, NB), NB)
        v = mixed_v[at, :] / wide(plen[at, :])
        centre = v - jnp.sum(v, axis=1, keepdims=True) * inv
        r = lax.rsqrt(jnp.sum(centre * centre, axis=1, keepdims=True) * inv + NORM_EPS)
        unit = centre * r
        mixed_v[at, :] = v
        xhat2[at, :] = unit
        norm2[at, :] = (unit * mgain).astype(bf16)
        rstd2[at, :] = jnp.broadcast_to(r, (NB, 128))
        glow[at, :] = gout_v[at, :].astype(bf16)

    each(segs // NB, norm_pooled)
    loads[1].wait()
    loads[2].wait()

    hb = 512
    n_hb = hidden // hb
    n_cols = chans // 128
    partner = dp + 1 - 2 * core

    def core_copy(j):
        at = pl.ds(pl.multiple_of(j * hb, hb), hb)
        return remote(gw.at[1 - core, :, at, :], rc.at[:, at, :], core_s.at[j], core_r.at[j], partner, me)

    def mlp_block(j):
        at_h = pl.ds(pl.multiple_of(j * hb, hb), hb)
        w_in, w_out = win_v[:, at_h], wout_v[at_h, :]
        n2, gl = norm2[...], glow[...]
        rows_v[0:segs, :] = mm(n2, w_in)
        rows_v[segs:2 * segs, :] = mm_last(gl, w_out)

        def act(i):
            start = pl.multiple_of(i * 16, 16)
            at, at2 = pl.ds(start, 16), pl.ds(start + segs, 16)
            h, ga = rows_v[at, :], rows_v[at2, :]
            h2 = h * h
            t = jnp.tanh(h * (GELU_A + (GELU_A * GELU_B) * h2))
            half_t = 0.5 + 0.5 * t
            slope = half_t + (0.5 * h) * (1.0 - t * t) * (GELU_A + (3.0 * GELU_A * GELU_B) * h2)
            at_b = pl.ds(pl.multiple_of(start + j * segs, 16), 16)
            rows_hl[at_b, :] = (h * half_t).astype(bf16)
            val_hl[at_b, :] = (ga * slope).astype(bf16)

        each(segs // 16, act)
        at_j = pl.ds(pl.multiple_of(j * segs, segs), segs)
        part_in, part_out = mm_first(val_hl[at_j, :], n2), mm_first(rows_hl[at_j, :], gl)
        for c in range(n_cols):
            gw[0, c, at_h, :] = part_in[:, c * 128:(c + 1) * 128]
            gw[1, c, at_h, :] = part_out[:, c * 128:(c + 1) * 128]
        core_copy(j).start()

    per = 256
    n_per = hb // per

    def y_send(j, o):
        yy = lax.rem(y + o, n_y)
        at = pl.ds(pl.multiple_of(j * hb, hb), hb)
        k = j * n_y + o - 1
        return remote(gw.at[core, yy, at, :], ry.at[o - 1, at, :], y_s.at[k], y_r.at[k], yy * 2 + core, me)

    def core_done(j):
        core_copy(j).wait_recv()

        def add_core(i):
            c, k = lax.div(i, n_per), lax.rem(i, n_per)
            at = pl.ds(pl.multiple_of(j * hb + k * per, per), per)
            gw[core, c, at, :] += rc[c, at, :]

        each(n_cols * n_per, add_core)
        each(n_y, lambda o: y_send(j, o).start(), 1)

    def mlp_step(j):
        mlp_block(j)

        @pl.when(j > 0)
        def _():
            core_done(j - 1)

    each(n_hb, mlp_step)
    gnorm[...] = sum(
        mm_last(val_hl[j * segs:(j + 1) * segs, :], win_v[:, j * hb:(j + 1) * hb]) for j in range(n_hb))

    small[...] = jnp.zeros(small.shape, f32)

    def norm_back(i):
        at = pl.ds(pl.multiple_of(i * NB, NB), NB)
        g, unit = gnorm[at, :], xhat2[at, :]
        prod = g * unit
        small[0:8, :] += fold8(prod)
        dx = g * mgain
        a = jnp.sum(dx, axis=1, keepdims=True) * inv
        b = jnp.sum(prod * mgain, axis=1, keepdims=True) * inv
        gp = gout_v[at, :] + wide(rstd2[at, :]) * (dx - a - unit * b)
        val_hi[at, :], val_lo[at, :] = split_hi_lo(gp / wide(plen[at, :]))

    each(segs // NB, norm_back)
    mgain_part = jnp.sum(small[0:8, :], axis=0, keepdims=True)
    gc[pl.ds(PAD, count), :] = mm(pool_t[...], val_hi[0:segs, :]) + mm(pool_t[...], val_lo[0:segs, :])
    for copy in halo(gc, 2):
        copy.start()

    core_done(n_hb - 1)

    n_back = count // CB

    def back_rows(i):
        base = pl.multiple_of(i * CB, CB)
        own = pl.ds(base + PAD, CB)
        here, unit = sid[own, :], xhat[own, :]
        gl = jnp.zeros((CB, chans), f32)
        around = gc[pl.ds(base, CB + 2 * PAD), :]
        for e in range(-half, half + 1):
            same = wide(ones_where(sid[pl.ds(base + PAD + e, CB), :] == here)) * rows_from(around, PAD + e, CB)
            gl = gl + taps[half - e:half - e + 1, :] * same
            gtap_acc[half - e] += fold8(unit * same)
        dx = gl * cgain
        a = jnp.sum(dx, axis=1, keepdims=True) * inv
        b = jnp.sum(dx * unit, axis=1, keepdims=True) * inv
        gs = gc[own, :] + wide(rstd[own, :]) * (dx - a - unit * b)
        at = pl.ds(base, CB)
        val_hi[at, :], val_lo[at, :] = split_hi_lo(gs)

    each(n_back - 1, back_rows, 1)
    for copy in halo(gc, 2):
        copy.wait_recv()
    each(2, lambda i: back_rows(i * (n_back - 1)))

    def sent_all(i):
        p = lax.rem(me + i, n_seq)
        row_out(p, outb, inb, row_s, row_r).wait_send()

    each(n_seq, sent_all, 1)
    slot_at = iota_f((slots, count), 0)

    def return_group(g):
        p0 = group_out(g)
        hot = ones_where(slot_at == srow[0:1, :] - (p0 * cap).astype(f32)).astype(bf16)
        made = mm(hot, val_hi[...]) + mm(hot, val_lo[...])
        outb[pl.ds(p0, group)] = made.reshape(group, cap, chans)
        launch(p0, inb2, back_s, back_r)

    if spare:
        hot = ones_where(
            jnp.broadcast_to(orow[0:1, :], (n_seq, count)) == iota_f((n_seq, count), 0)).astype(bf16)
        hop_send(mm(hot, val_hi[...]) + mm(hot, val_lo[...]), *ret1)
        each(n_groups // 2, return_group)
        high, low = hop_read(*ret1)
        hop_send(mm_first(pass_on, high) + mm_first(pass_on, low), *ret2)
        each(n_groups, return_group, n_groups // 2)
    else:
        each(n_groups, return_group)

    for d in range(2 * half + 1):
        small[d:d + 1, :] = jnp.sum(gtap_acc[d], axis=0, keepdims=True)
    small[7:8, :] = mgain_part
    small[8:16, :] = jnp.broadcast_to(misfit, (8, chans))
    rs1[dp] = small[...]

    def s1_send(o):
        to = lax.rem(dp + o, n_dp)
        return remote(small, rs1.at[dp], s1_s.at[to], s1_r.at[dp], to, me)

    def s1_recv(o):
        to = lax.rem(dp + o, n_dp)
        return remote(small, rs1.at[to], s1_s.at[to], s1_r.at[to], to, me)

    each(n_dp, lambda o: s1_send(o).start(), 1)

    mixed_v[...] += sum(
        mm(rows_hl[j * segs:(j + 1) * segs, :], wout_v[j * hb:(j + 1) * hb, :]) for j in range(n_hb))
    store_mixed = pltpu.make_async_copy(mixed_v, mixed_hbm, ld_sem.at[4])
    store_mixed.start()

    share = hidden // n_seq
    z_per = n_z // n_hb

    def x_send(j, o):
        xx = lax.rem(x + o, NX)
        at, k = pl.ds(j * z_per, z_per), j * NX + o - 1
        return remote(wx.at[xx, at], rx.at[o - 1, at], x_s.at[k], x_r.at[k], dp, z * NX + xx)

    def y_done(j):
        each(n_y, lambda o: y_send(j, o).wait_recv(), 1)

        def add_y(i):
            zz, xx = j * z_per + lax.div(i, NX), lax.rem(i, NX)
            at = pl.ds(pl.multiple_of((zz * NX + xx) * share, share), share)
            total = gw[core, y, at, :]
            for o in range(n_y - 1):
                total = total + ry[o, at, :]
            wx[xx, zz] = total

        each(z_per * NX, add_y)
        each(NX, lambda o: x_send(j, o).start(), 1)

    each(n_hb, y_done)
    each(n_dp, lambda o: s1_recv(o).wait_recv(), 1)
    total = rs1[0]
    for i in range(1, n_dp):
        total = total + rs1[i]
    rs2[x] = total

    def s2_send(o):
        xx = lax.rem(x + o, NX)
        return remote(rs2.at[x], rs2.at[x], s2_s.at[xx], s2_r.at[x], dp, z * NX + xx)

    def s2_recv(o):
        xx = lax.rem(x + o, NX)
        return remote(rs2.at[x], rs2.at[xx], s2_s.at[xx], s2_r.at[xx], dp, z * NX + xx)

    each(NX, lambda o: s2_send(o).start(), 1)
    each(n_hb, lambda j: each(NX, lambda o: x_send(j, o).wait_recv(), 1))

    def add_x(zz):
        total = wx[x, zz]
        for o in range(NX - 1):
            total = total + rx[o, zz]
        wz[zz] = total

    each(n_z, add_x)
    each(NX, lambda o: s2_recv(o).wait_recv(), 1)
    total = rs2[0]
    for i in range(1, NX):
        total = total + rs2[i]
    rs3[z] = total

    def z_send(o):
        zz = lax.rem(z + o, n_z)
        return remote(wz.at[zz], rz.at[o - 1], z_s.at[o - 1], z_r.at[o - 1], dp, zz * NX + x)

    def s3_send(o):
        zz = lax.rem(z + o, n_z)
        return remote(rs3.at[z], rs3.at[z], s3_s.at[zz], s3_r.at[z], dp, zz * NX + x)

    def s3_recv(o):
        zz = lax.rem(z + o, n_z)
        return remote(rs3.at[z], rs3.at[zz], s3_s.at[zz], s3_r.at[zz], dp, zz * NX + x)

    each(n_z, lambda o: z_send(o).start(), 1)
    each(n_z, lambda o: s3_send(o).start(), 1)
    each(n_z, lambda o: z_send(o).wait_recv(), 1)
    total = wz[z]
    for o in range(n_z - 1):
        total = total + rz[o]
    fin[core, y] = total

    def f_send(o):
        to = lax.rem(dp + o, n_dp)
        return remote(fin.at[core, y], fin.at[core, y], f_s.at[to], f_r.at[dp], to, me)

    def f_recv(o):
        to = lax.rem(dp + o, n_dp)
        part = fin.at[lax.rem(to, 2), lax.div(to, 2)]
        return remote(fin.at[core, y], part, f_s.at[to], f_r.at[to], to, me)

    each(n_dp, lambda o: f_send(o).start(), 1)
    each(n_z, lambda o: s3_recv(o).wait_recv(), 1)
    total = rs3[0]
    for i in range(1, n_z):
        total = total + rs3[i]
    gtaps_ref[...] = total[0:2 * half + 1, :] * cgain
    gcg_ref[...] = jnp.sum(total[0:2 * half + 1, :] * taps, axis=0, keepdims=True)
    gmg_ref[...] = total[7:8, :]
    misfit_ref[...] = total[8:16, 0:128]

    def clear_rows(i):
        rows_v[pl.ds(pl.multiple_of(i * 8, 8), 8), :] = jnp.zeros((8, chans), f32)

    each(count // 8, clear_rows)

    def settle_group(g):
        p0 = group_in(g)
        arrive(p0, inb2, back_s, back_r)
        high, low = split_hi_lo(inb2[pl.ds(p0, group)].reshape(slots, chans))
        hot = pick[pl.ds(pl.multiple_of(p0 * cap, 16), slots), :]
        rows_v[...] += mm_first(hot, high) + mm_first(hot, low)

    each(n_groups, settle_group)
    if spare:
        high, low = hop_read(*ret2)
        rows_v[...] += mm_first(pick2[...], high) + mm_first(pick2[...], low)
    store_rows = pltpu.make_async_copy(rows_v, grows_hbm, ld_sem.at[5])
    store_rows.start()

    each(n_dp, lambda o: f_recv(o).wait_recv(), 1)
    gwout_ref[...] = jnp.concatenate([fin[1, c] for c in range(n_cols)], axis=1)
    gwin_ref[...] = jnp.concatenate([fin[0, c] for c in range(n_cols)], axis=1)

    each(n_seq, lambda i: send_list(i).wait_send(), 1)

    def back_sent(i):
        p = lax.rem(me + i, n_seq)
        row_out(p, outb, inb2, back_s, back_r).wait_send()

    each(n_seq, back_sent, 1)
    for copy in halo(ser, 0) + halo(gc, 2):
        copy.wait_send()
    each(n_hb, lambda j: core_copy(j).wait_send())
    each(n_hb, lambda j: each(n_y, lambda o: y_send(j, o).wait_send(), 1))
    each(n_hb, lambda j: each(NX, lambda o: x_send(j, o).wait_send(), 1))
    each(n_z, lambda o: z_send(o).wait_send(), 1)
    each(n_dp, lambda o: s1_send(o).wait_send(), 1)
    each(NX, lambda o: s2_send(o).wait_send(), 1)
    each(n_z, lambda o: s3_send(o).wait_send(), 1)
    each(n_dp, lambda o: f_send(o).wait_send(), 1)
    if spare:
        for hop in (hop1, hop2, ret1, ret2):
            each(n_seq, lambda i: hop_out(i, *hop).wait_send(), 1)
    store_mixed.wait()
    store_rows.wait()


def copy_out(*refs):
    count = len(refs) // 2
    sems = refs[-1]
    copies, used = [], 0
    for src, dst in zip(refs[:count], refs[count:2 * count]):
        pieces = 4 if src.shape[0] % 128 == 0 and src.shape[1] % 512 == 0 else 1
        step = src.shape[0] // pieces
        for k in range(pieces):
            at = pl.ds(k * step, step)
            copies.append(pltpu.make_async_copy(
                src.at[at] if pieces > 1 else src, dst.at[at] if pieces > 1 else dst, sems.at[used]))
            used += 1
    for copy in copies:
        copy.start()
    for copy in copies:
        copy.wait()


def make_body(n_dp, n_seq):
    n_y, n_z = n_dp // 2, n_seq // NX

    def body(point_rows, serial_order, scene_counts, pool_counts, conv_gain, conv_kernel, mixer_gain,
             weight_in, weight_out, grad_out):
        count, chans = point_rows.shape
        segs = grad_out.shape[0]
        hidden = weight_out.shape[0]
        even = count // n_seq
        share = hidden // n_seq
        pads = count + 2 * PAD
        cols = chans // 128
        V = pltpu.VMEM
        D = lambda n: pltpu.SemaphoreType.DMA((n,))
        any_spec = pl.BlockSpec(memory_space=pl.ANY)
        vmem = pl.BlockSpec(memory_space=pltpu.VMEM)
        shape = jax.ShapeDtypeStruct
        scratch = lambda cap: [
            V((count, chans), f32), V((2 * count, chans), bf16),
            V((n_seq, 8, 128), f32), V((n_seq, 8, 128), f32), V((count, 128), bf16),
            V((count, 128), f32), V((8, count), f32), V((128, n_seq * 8), f32), V((n_seq * cap, count), bf16),
            V((n_seq, cap, chans), f32), V((n_seq, cap, chans), f32), V((n_seq, cap, chans), f32),
            V((pads, chans), f32), V((pads, chans), f32), V((pads, 128), f32), V((pads, 128), f32),
            V((2 * count, chans), bf16),
            V((segs, count), bf16), V((count, segs), bf16), V((segs, 128), f32),
            V((segs, chans), f32), V((segs, chans), bf16), V((segs, chans), f32), V((segs, chans), f32),
            V((segs, chans), bf16), V((segs, chans), f32), V((segs, 128), f32),
            V((chans, hidden), bf16), V((hidden, chans), bf16),
            V((2, cols, hidden, 128), f32), V((cols, hidden, 128), f32), V((n_y - 1, hidden, 128), f32),
            V((NX, n_z, share, 128), f32), V((NX - 1, n_z, share, 128), f32),
            V((n_z, share, 128), f32), V((n_z - 1, share, 128), f32), V((2, cols, share, 128), f32),
            V((pads, chans), f32), V((8, 8, chans), f32), V((16, chans), f32),
            V((n_dp, 16, chans), f32), V((NX, 16, chans), f32), V((n_z, 16, chans), f32),
            D(6), D(n_seq), D(n_seq), D(n_seq), D(n_seq), D(n_seq), D(n_seq), D(4), D(4),
            D(hidden // 512), D(hidden // 512), D(4 * n_y), D(4 * n_y), D(4 * NX), D(4 * NX), D(n_z), D(n_z),
            D(n_dp), D(n_dp), D(NX), D(NX), D(n_z), D(n_z), D(n_dp), D(n_dp),
        ]
        hop = [V((n_seq, 1, chans), f32)] * 8
        extra = [V((count, 128), f32), V((8, count), f32), V((n_seq, count), bf16)] + hop + [D(n_seq)] * 8

        def call(cap, spare, ident, name):
            return pl.pallas_call(
                lambda *refs: kernel(n_dp, n_seq, cap, spare, *refs),
                out_shape=(
                    shape((segs, chans), f32), shape((count, chans), f32), shape((share, chans), f32),
                    shape((share, chans), f32), shape(conv_kernel.shape, f32), shape((1, chans), f32),
                    shape((1, chans), f32), shape((8, 128), f32),
                ),
                in_specs=[any_spec] + [vmem] * 6 + [any_spec] * 3,
                out_specs=(any_spec, any_spec, vmem, vmem, vmem, vmem, vmem, vmem),
                scratch_shapes=scratch(cap) + (extra if spare else []),
                compiler_params=pltpu.CompilerParams(
                    collective_id=ident, has_side_effects=True, vmem_limit_bytes=62 * 1024 * 1024),
                name=name,
            )(
                point_rows, serial_order, scene_counts, pool_counts.reshape(1, segs), conv_gain[None], conv_kernel,
                mixer_gain[None], weight_in, weight_out, grad_out,
            )

        outs = call(even, even // 2, 0, "window_even")
        outs = lax.cond(
            outs[7][0, 0] > 0.0, lambda: call(even + even // 2, 0, 1, "window_full")[:7], lambda: outs[:7])
        mixed, grows, gwin, gwout, gtaps, gcg, gmg = pl.pallas_call(
            copy_out,
            out_shape=tuple(shape(value.shape, f32) for value in outs),
            in_specs=[any_spec] * 7,
            out_specs=(any_spec,) * 7,
            scratch_shapes=[D(16)],
            name="outputs",
        )(*outs)
        return mixed, grows, gwin.T, gwout, gtaps, gcg[0], gmg[0]

    return body


def solution(mesh):
    return jax.shard_map(
        make_body(mesh.shape["dp"], mesh.shape["seq"]),
        mesh=mesh,
        in_specs=(
            P(("dp", "seq"), None), P("dp", "seq"), P("dp", None), P("dp", "seq", None), P(), P(), P(), P(), P(),
            P(("dp", "seq"), None),
        ),
        out_specs=(
            P(("dp", "seq"), None), P(("dp", "seq"), None), P(None, "seq"), P("seq", None), P(), P(), P(),
        ),
        check_vma=False,
    )
```

```python
import jax
import jax.numpy as jnp
from jax import lax
from jax.experimental import pallas as pl
from jax.experimental.pallas import tpu as pltpu
from jax.sharding import PartitionSpec as P

NORM_EPS = 1e-05
MESH = pl.DeviceIdType.MESH
f32, bf16 = jnp.float32, jnp.bfloat16
NX = 4
CH = 32
NB = 128
CB = 64
PAD = 8
GELU_A = 0.7978845608028654
GELU_B = 0.044715


def iota_f(shape, dim):
    return lax.broadcasted_iota(jnp.int32, shape, dim).astype(f32)


def ones_where(mask):
    return jnp.where(mask, 1.0, 0.0)


def split_hi_lo(value):
    high = value.astype(bf16)
    return high, (value - high.astype(f32)).astype(bf16)


def mm(a, b):
    return jnp.dot(a, b, preferred_element_type=f32)


def mm_last(a, b):
    return lax.dot_general(a, b, (((1,), (1,)), ((), ())), preferred_element_type=f32)


def mm_first(a, b):
    return lax.dot_general(a, b, (((0,), (0,)), ((), ())), preferred_element_type=f32)


def fold8(value):
    return jnp.sum(value.reshape(value.shape[0] // 8, 8, value.shape[1]), axis=0)


def rows_from(window, offset, count):
    size = window.shape[0]
    return pltpu.roll(window, (size - offset) % size, 0)[0:count]


def wide(value):
    return jnp.concatenate([value] * 4, axis=1)


def kernel(
    n_dp, n_seq, cap, spare,
    rows_hbm, order_ref, scene_ref, pool_ref, cgain_ref, taps_ref, mgain_ref, win_hbm, wout_hbm, gout_hbm,
    mixed_hbm, grows_hbm, gwin_ref, gwout_ref, gtaps_ref, gcg_ref, gmg_ref, misfit_ref,
    rows_v, rows_hl, list_s, list_r, kmat, scol, srow, tcol, pick,
    outb, inb, inb2, ser, xhat, rstd, sid, val_hl,
    pool_m, pool_t, plen, gout_v, glow, mixed_v, xhat2, norm2, gnorm, rstd2,
    win_v, wout_v, gw, rc, ry, wx, rx, wz, rz, fin, gc, gtap_acc, small, rs1, rs2, rs3,
    ld_sem, idx_s, idx_r, row_s, row_r, back_s, back_r, halo_s, halo_r,
    core_s, core_r, y_s, y_r, x_s, x_r, z_s, z_r, s1_s, s1_r, s2_s, s2_r, s3_s, s3_r, f_s, f_r, *extra,
):
    if spare:
        ocol, orow, pick2, hop_a, hop_b, hop_c, hop_d, ret_a, ret_b, ret_c, ret_d = extra[:11]
        hop1_s, hop1_r, hop2_s, hop2_r, ret1_s, ret1_r, ret2_s, ret2_r = extra[11:]
    count, chans = rows_v.shape
    segs = mixed_v.shape[0]
    rows_hi, rows_lo = rows_hl.at[pl.ds(0, count)], rows_hl.at[pl.ds(count, count)]
    val_hi, val_lo = val_hl.at[pl.ds(0, count)], val_hl.at[pl.ds(count, count)]
    hidden = wout_v.shape[0]
    n_y, n_z = n_dp // 2, n_seq // NX
    group = 8
    n_groups = n_seq // group
    slots = group * cap
    dp, me = lax.axis_index("dp"), lax.axis_index("seq")
    y, core = lax.div(dp, 2), lax.rem(dp, 2)
    z, x = lax.div(me, NX), lax.rem(me, NX)
    my_group = lax.div(me, group)

    def remote(src, dst, send, recv, to_dp, to_seq):
        return pltpu.make_async_remote_copy(
            src_ref=src, dst_ref=dst, send_sem=send, recv_sem=recv,
            device_id=(to_dp, to_seq), device_id_type=MESH,
        )

    def each(n, fn, start=0):
        def step(i, carry):
            fn(i)
            return carry
        lax.fori_loop(start, n, step, 0)

    loads = [
        pltpu.make_async_copy(rows_hbm, rows_v, ld_sem.at[0]),
        pltpu.make_async_copy(win_hbm, win_v, ld_sem.at[1]),
        pltpu.make_async_copy(wout_hbm, wout_v, ld_sem.at[2]),
        pltpu.make_async_copy(gout_hbm, gout_v, ld_sem.at[3]),
    ]
    for load in loads:
        load.start()

    barrier = pltpu.get_barrier_semaphore()
    each(n_seq, lambda i: pl.semaphore_signal(
        barrier, inc=1, device_id=(dp, lax.rem(me + i, n_seq)), device_id_type=MESH), 1)
    each(n_dp, lambda i: pl.semaphore_signal(
        barrier, inc=1, device_id=(lax.rem(dp + i, n_dp), me), device_id_type=MESH), 1)

    order = order_ref[...]
    shift = count.bit_length() - 1
    owner = (order >> shift).astype(f32)
    local = order & (count - 1)
    local_hi = (local >> 5).astype(f32)
    local_lo = (local & 31).astype(f32)
    owner_col = jnp.transpose(jnp.broadcast_to(owner, (128, count)))
    lane = iota_f((128, 128), 1)
    below = ones_where(iota_f((128, 128), 0) > lane).astype(bf16)
    before = jnp.zeros((1, 128), f32)
    for b in range(count // 128):
        own_b = owner_col[b * 128:(b + 1) * 128]
        hot = ones_where(own_b == lane)
        ranks = mm(below, hot.astype(bf16)) + before
        before = before + jnp.sum(hot, axis=0, keepdims=True)
        rank = jnp.broadcast_to(jnp.sum(hot * ranks, axis=1, keepdims=True), (128, 128))
        slot = own_b * cap + rank
        if spare:
            via = rank + (me + 1 - cap).astype(f32)
            via = jnp.where(via >= n_seq, via - n_seq, via)
            ocol[b * 128:(b + 1) * 128, :] = jnp.where(rank >= cap, via, -1.0)
            slot = jnp.where(rank >= cap, -1.0, slot)
        scol[b * 128:(b + 1) * 128, :] = slot
        kmat[b * 128:(b + 1) * 128, :] = ones_where(rank == lane).astype(bf16)
    srow[...] = jnp.transpose(scol[...])[0:8, :]
    if spare:
        orow[...] = jnp.transpose(ocol[...])[0:8, :]
    owner_hot = ones_where(jnp.broadcast_to(owner, (n_seq, count)) == iota_f((n_seq, count), 0))
    kval = kmat[...]
    lists = (
        mm((owner_hot * local_hi).astype(bf16), kval) * 32.0
        + mm((owner_hot * local_lo).astype(bf16), kval)
        + mm(owner_hot.astype(bf16), kval)
        - 1.0
    )
    misfit = jnp.zeros((1, 1), f32)
    if spare:
        over = ones_where(before > cap)
        over_n = jnp.sum(jnp.maximum(before - cap, 0.0), axis=1, keepdims=True)
        over_from = jnp.sum(over * lane[0:1], axis=1, keepdims=True)
        misfit = misfit + ones_where(jnp.sum(over, axis=1, keepdims=True) > 1.0)
        place = iota_f((n_seq, 128), 0) - (me + 1).astype(f32)
        place = jnp.where(place < 0.0, place + n_seq, place)
        passed = jnp.where(place < over_n, over_from, -1.0)
        lists = jnp.where(iota_f((n_seq, 128), 1) == 64.0, passed, lists)
    for p in range(n_seq):
        list_s[p] = jnp.broadcast_to(lists[p:p + 1, :], (8, 128))
    list_r[me] = list_s[me]

    pl.semaphore_wait(barrier, n_seq - 1 + n_dp - 1)

    def send_list(i):
        p = lax.rem(me + i, n_seq)
        return remote(list_s.at[p], list_r.at[me], idx_s.at[p], idx_r.at[me], dp, p)

    def recv_list(i):
        p = lax.rem(me + i, n_seq)
        return remote(list_s.at[p], list_r.at[p], idx_s.at[p], idx_r.at[p], dp, p)

    each(n_seq, lambda i: send_list(i).start(), 1)

    loads[0].wait()

    def split_rows(i):
        at = pl.ds(pl.multiple_of(i * CH, CH), CH)
        rows_hi[at, :], rows_lo[at, :] = split_hi_lo(rows_v[at, :])

    each(count // CH, split_rows)
    each(n_seq, lambda i: recv_list(i).wait_recv(), 1)

    tcol[...] = jnp.transpose(list_r[...].reshape(n_seq * 8, 128))

    def hop_out(i, src, dst, send, recv):
        p = lax.rem(me + i, n_seq)
        return remote(src.at[p], dst.at[me], send.at[p], recv.at[me], dp, p)

    def hop_in(i, src, dst, send, recv):
        p = lax.rem(me + i, n_seq)
        return remote(src.at[p], dst.at[p], send.at[p], recv.at[p], dp, p)

    def hop_send(value, src, dst, send, recv):
        for p in range(n_seq):
            src[p] = value[p:p + 1, :]
        dst[me] = src[me]
        each(n_seq, lambda i: hop_out(i, src, dst, send, recv).start(), 1)

    def hop_read(src, dst, send, recv):
        each(n_seq, lambda i: hop_in(i, src, dst, send, recv).wait_recv(), 1)
        return split_hi_lo(jnp.concatenate([dst[p] for p in range(n_seq)], axis=0))

    if spare:
        flat = list_r[...].reshape(n_seq * 8, 128)
        wanted = jnp.max(flat, axis=0, keepdims=True)
        blocks = lax.broadcasted_iota(jnp.int32, (1, n_seq * 8), 1)
        busy = tcol[cap:cap + 1, :] >= 0.0
        over_to = jnp.max(jnp.where(busy, (blocks >> 3).astype(f32), -1.0), axis=1, keepdims=True)
        misfit = misfit + ones_where(jnp.sum(ones_where(busy), axis=1, keepdims=True) > 8.0)
        place = iota_f((n_seq, 128), 0) - 1.0 - over_to
        place = jnp.where(place < 0.0, place + n_seq, place)
        col = jnp.sum(jnp.where(iota_f((n_seq, 128), 1) == place + cap, wanted + 1.0, 0.0), axis=1, keepdims=True) - 1.0
        pick2[...] = ones_where(jnp.broadcast_to(col, (n_seq, count)) == iota_f((n_seq, count), 1)).astype(bf16)
        hop1 = (hop_a, hop_b, hop1_s, hop1_r)
        hop2 = (hop_c, hop_d, hop2_s, hop2_r)
        ret1 = (ret_a, ret_b, ret1_s, ret1_r)
        ret2 = (ret_c, ret_d, ret2_s, ret2_r)
        hop_send(mm(pick2[...], rows_hi[...]) + mm(pick2[...], rows_lo[...]), *hop1)
        rows_of = jnp.max(list_r[...], axis=1)
        passed_from = jnp.sum(
            jnp.where(iota_f((n_seq, 128), 1) == 64.0, rows_of, 0.0), axis=1, keepdims=True)
        pass_on = ones_where(
            jnp.broadcast_to(passed_from, (n_seq, n_seq)) == iota_f((n_seq, n_seq), 1)).astype(bf16)

    def row_out(p, src, dst, send, recv):
        return remote(src.at[p], dst.at[me], send.at[p], recv.at[me], dp, p)

    def row_self(src, dst, recv):
        return pltpu.make_async_copy(src.at[me], dst.at[me], recv.at[me])

    def launch(p0, dst, send, recv):
        def one(i):
            p = p0 + i

            @pl.when(p != me)
            def _():
                row_out(p, outb, dst, send, recv).start()

            @pl.when(p == me)
            def _():
                row_self(outb, dst, recv).start()
        each(group, one)

    def arrive(p0, dst, send, recv):
        def one(i):
            p = p0 + i

            @pl.when(p != me)
            def _():
                remote(outb.at[p], dst.at[p], send.at[p], recv.at[p], dp, p).wait_recv()

            @pl.when(p == me)
            def _():
                row_self(outb, dst, recv).wait()
        each(group, one)

    def group_out(g):
        return group * lax.rem(my_group + g, n_groups)

    def group_in(g):
        return group * lax.rem(my_group + n_groups - g, n_groups)

    tlane = lax.broadcasted_iota(jnp.int32, (cap, n_seq * 8), 1)
    rlane = iota_f((cap, count), 1)

    def gather_group(g):
        p0 = group_out(g)

        def one(i):
            p = p0 + i
            col = jnp.sum(jnp.where(tlane == p * 8, tcol[0:cap, :], 0.0), axis=1, keepdims=True)
            pick[pl.ds(pl.multiple_of(p * cap, 16), cap), :] = ones_where(
                jnp.broadcast_to(col, (cap, count)) == rlane).astype(bf16)
        each(group, one)
        hot = pick[pl.ds(pl.multiple_of(p0 * cap, 16), slots), :]
        made = mm(hot, rows_hi[...]) + mm(hot, rows_lo[...])
        outb[pl.ds(p0, group)] = made.reshape(group, cap, chans)
        launch(p0, inb, row_s, row_r)

    if spare:
        each(n_groups // 2, gather_group)
        high, low = hop_read(*hop1)
        hop_send(mm(pass_on, high) + mm(pass_on, low), *hop2)
        each(n_groups, gather_group, n_groups // 2)
    else:
        each(n_groups, gather_group)

    scene_n = scene_ref.shape[1]
    upto = ones_where(iota_f((scene_n, scene_n), 0) <= iota_f((scene_n, scene_n), 1))
    scene_ends = lax.dot_general(
        jnp.broadcast_to(scene_ref[...].astype(f32), (8, scene_n)), upto, (((1,), (0,)), ((), ())),
        precision=lax.Precision.HIGHEST, preferred_element_type=f32)[0:1, :]
    first_pos = (me * count - PAD).astype(f32)

    def scenes(i):
        start = pl.multiple_of(i * 8, 8)
        pos = iota_f((8, scene_n), 0) + (first_pos + start.astype(f32))
        ids = jnp.sum(ones_where(pos >= scene_ends), axis=1, keepdims=True)
        ids = jnp.where(pos[:, 0:1] < 0.0, -1.0, ids)
        sid[pl.ds(start, 8), :] = jnp.broadcast_to(ids, (8, 128))

    each(sid.shape[0] // 8, scenes)

    lens = jnp.broadcast_to(pool_ref[...].astype(f32), (128, segs))
    len_col = jnp.transpose(lens)
    plen[...] = len_col
    tri_rows, tri_cols = iota_f((segs, segs), 0), iota_f((segs, segs), 1)
    end_col = mm(ones_where(tri_cols <= tri_rows).astype(bf16), len_col.astype(bf16))
    end_row = mm(lens[0:8].astype(bf16), ones_where(tri_rows <= tri_cols).astype(bf16))[0:1, :]
    start_col = end_col - len_col
    start_row = end_row - lens[0:1]
    for t in range(count // 128):
        at_pos = iota_f((segs, 128), 1) + float(t * 128)
        pool_m[:, t * 128:(t + 1) * 128] = ones_where((at_pos >= start_col) & (at_pos < end_col)).astype(bf16)

    def pool_rows(i):
        start = pl.multiple_of(i * CH, CH)
        at_pos = iota_f((CH, segs), 0) + start.astype(f32)
        pool_t[pl.ds(start, CH), :] = ones_where((at_pos >= start_row) & (at_pos < end_row)).astype(bf16)

    each(count // CH, pool_rows)

    def clear(i):
        ser[pl.ds(pl.multiple_of(i * 8 + PAD, 8), 8), :] = jnp.zeros((8, chans), f32)

    each(count // 8, clear)
    gtap_acc[...] = jnp.zeros(gtap_acc.shape, f32)

    slane = iota_f((count, 128), 1)

    def place_group(g):
        p0 = group_in(g)
        arrive(p0, inb, row_s, row_r)
        high, low = split_hi_lo(inb[pl.ds(p0, group)].reshape(slots, chans))
        at_slot = scol[...] - (p0 * cap).astype(f32)
        hot = jnp.concatenate(
            [ones_where(at_slot == slane + float(128 * t)).astype(bf16) for t in range(slots // 128)], axis=1)
        ser[pl.ds(PAD, count), :] += mm(hot, high) + mm(hot, low)

    each(n_groups, place_group)
    if spare:
        high, low = hop_read(*hop2)
        hot = ones_where(ocol[:, 0:n_seq] == iota_f((count, n_seq), 1)).astype(bf16)
        ser[pl.ds(PAD, count), :] += mm(hot, high) + mm(hot, low)

    right, left = lax.rem(me + 1, n_seq), lax.rem(me + n_seq - 1, n_seq)

    def halo(buf, k):
        return (
            remote(buf.at[pl.ds(count, PAD)], buf.at[pl.ds(0, PAD)], halo_s.at[k], halo_r.at[k], dp, right),
            remote(buf.at[pl.ds(PAD, PAD)], buf.at[pl.ds(count + PAD, PAD)], halo_s.at[k + 1], halo_r.at[k + 1],
                   dp, left),
        )

    for copy in halo(ser, 0):
        copy.start()

    inv = 1.0 / chans

    def norm_rows(start, rows):
        at = pl.ds(start, rows)
        v = ser[at, :]
        centre = v - jnp.sum(v, axis=1, keepdims=True) * inv
        r = lax.rsqrt(jnp.sum(centre * centre, axis=1, keepdims=True) * inv + NORM_EPS)
        xhat[at, :] = centre * r
        rstd[at, :] = jnp.broadcast_to(r, (rows, 128))

    each(count // NB, lambda i: norm_rows(pl.multiple_of(i * NB + PAD, 8), NB))
    half = taps_ref.shape[0] // 2
    taps = taps_ref[...]
    cgain = cgain_ref[...]
    taps_gain = taps * cgain

    def conv_rows(i):
        base = pl.multiple_of(i * CH, CH)
        here = sid[pl.ds(base + PAD, CH), :]
        total = ser[pl.ds(base + PAD, CH), :]
        around = xhat[pl.ds(base, CH + 2 * PAD), :]
        for d in range(2 * half + 1):
            same = wide(ones_where(sid[pl.ds(base + PAD + d - half, CH), :] == here))
            total = total + taps_gain[d:d + 1, :] * (same * rows_from(around, PAD + d - half, CH))
        at = pl.ds(base, CH)
        val_hi[at, :], val_lo[at, :] = split_hi_lo(total)

    n_chunks = count // CH
    each(n_chunks - 1, conv_rows, 1)
    for copy in halo(ser, 0):
        copy.wait_recv()
    norm_rows(0, PAD)
    norm_rows(count + PAD, PAD)
    each(2, lambda i: conv_rows(i * (n_chunks - 1)))

    mixed_v[...] = mm(pool_m[...], val_hi[...]) + mm(pool_m[...], val_lo[...])
    mgain = mgain_ref[...]
    loads[3].wait()

    def norm_pooled(i):
        at = pl.ds(pl.multiple_of(i * NB, NB), NB)
        v = mixed_v[at, :] / wide(plen[at, :])
        centre = v - jnp.sum(v, axis=1, keepdims=True) * inv
        r = lax.rsqrt(jnp.sum(centre * centre, axis=1, keepdims=True) * inv + NORM_EPS)
        unit = centre * r
        mixed_v[at, :] = v
        xhat2[at, :] = unit
        norm2[at, :] = (unit * mgain).astype(bf16)
        rstd2[at, :] = jnp.broadcast_to(r, (NB, 128))
        glow[at, :] = gout_v[at, :].astype(bf16)

    each(segs // NB, norm_pooled)
    loads[1].wait()
    loads[2].wait()

    hb = 512
    n_hb = hidden // hb
    n_cols = chans // 128
    partner = dp + 1 - 2 * core

    def core_copy(j):
        at = pl.ds(pl.multiple_of(j * hb, hb), hb)
        return remote(gw.at[1 - core, :, at, :], rc.at[:, at, :], core_s.at[j], core_r.at[j], partner, me)

    def mlp_block(j):
        at_h = pl.ds(pl.multiple_of(j * hb, hb), hb)
        w_in, w_out = win_v[:, at_h], wout_v[at_h, :]
        n2, gl = norm2[...], glow[...]
        rows_v[0:segs, :] = mm(n2, w_in)
        rows_v[segs:2 * segs, :] = mm_last(gl, w_out)

        def act(i):
            start = pl.multiple_of(i * 16, 16)
            at, at2 = pl.ds(start, 16), pl.ds(start + segs, 16)
            h, ga = rows_v[at, :], rows_v[at2, :]
            h2 = h * h
            t = jnp.tanh(h * (GELU_A + (GELU_A * GELU_B) * h2))
            half_t = 0.5 + 0.5 * t
            slope = half_t + (0.5 * h) * (1.0 - t * t) * (GELU_A + (3.0 * GELU_A * GELU_B) * h2)
            at_b = pl.ds(pl.multiple_of(start + j * segs, 16), 16)
            rows_hl[at_b, :] = (h * half_t).astype(bf16)
            val_hl[at_b, :] = (ga * slope).astype(bf16)

        each(segs // 16, act)
        at_j = pl.ds(pl.multiple_of(j * segs, segs), segs)
        part_in, part_out = mm_first(val_hl[at_j, :], n2), mm_first(rows_hl[at_j, :], gl)
        for c in range(n_cols):
            gw[0, c, at_h, :] = part_in[:, c * 128:(c + 1) * 128]
            gw[1, c, at_h, :] = part_out[:, c * 128:(c + 1) * 128]
        core_copy(j).start()

    per = 256
    n_per = hb // per

    def y_send(j, o):
        yy = lax.rem(y + o, n_y)
        at = pl.ds(pl.multiple_of(j * hb, hb), hb)
        k = j * n_y + o - 1
        return remote(gw.at[core, yy, at, :], ry.at[o - 1, at, :], y_s.at[k], y_r.at[k], yy * 2 + core, me)

    def core_done(j):
        core_copy(j).wait_recv()

        def add_core(i):
            c, k = lax.div(i, n_per), lax.rem(i, n_per)
            at = pl.ds(pl.multiple_of(j * hb + k * per, per), per)
            gw[core, c, at, :] += rc[c, at, :]

        each(n_cols * n_per, add_core)
        each(n_y, lambda o: y_send(j, o).start(), 1)

    def mlp_step(j):
        mlp_block(j)

        @pl.when(j > 0)
        def _():
            core_done(j - 1)

    each(n_hb, mlp_step)
    gnorm[...] = sum(
        mm_last(val_hl[j * segs:(j + 1) * segs, :], win_v[:, j * hb:(j + 1) * hb]) for j in range(n_hb))

    small[...] = jnp.zeros(small.shape, f32)

    def norm_back(i):
        at = pl.ds(pl.multiple_of(i * NB, NB), NB)
        g, unit = gnorm[at, :], xhat2[at, :]
        prod = g * unit
        small[0:8, :] += fold8(prod)
        dx = g * mgain
        a = jnp.sum(dx, axis=1, keepdims=True) * inv
        b = jnp.sum(prod * mgain, axis=1, keepdims=True) * inv
        gp = gout_v[at, :] + wide(rstd2[at, :]) * (dx - a - unit * b)
        val_hi[at, :], val_lo[at, :] = split_hi_lo(gp / wide(plen[at, :]))

    each(segs // NB, norm_back)
    mgain_part = jnp.sum(small[0:8, :], axis=0, keepdims=True)
    gc[pl.ds(PAD, count), :] = mm(pool_t[...], val_hi[0:segs, :]) + mm(pool_t[...], val_lo[0:segs, :])
    for copy in halo(gc, 2):
        copy.start()

    core_done(n_hb - 1)

    n_back = count // CB

    def back_rows(i):
        base = pl.multiple_of(i * CB, CB)
        own = pl.ds(base + PAD, CB)
        here, unit = sid[own, :], xhat[own, :]
        gl = jnp.zeros((CB, chans), f32)
        around = gc[pl.ds(base, CB + 2 * PAD), :]
        for e in range(-half, half + 1):
            same = wide(ones_where(sid[pl.ds(base + PAD + e, CB), :] == here)) * rows_from(around, PAD + e, CB)
            gl = gl + taps[half - e:half - e + 1, :] * same
            gtap_acc[half - e] += fold8(unit * same)
        dx = gl * cgain
        a = jnp.sum(dx, axis=1, keepdims=True) * inv
        b = jnp.sum(dx * unit, axis=1, keepdims=True) * inv
        gs = gc[own, :] + wide(rstd[own, :]) * (dx - a - unit * b)
        at = pl.ds(base, CB)
        val_hi[at, :], val_lo[at, :] = split_hi_lo(gs)

    each(n_back - 1, back_rows, 1)
    for copy in halo(gc, 2):
        copy.wait_recv()
    each(2, lambda i: back_rows(i * (n_back - 1)))

    def sent_all(i):
        p = lax.rem(me + i, n_seq)
        row_out(p, outb, inb, row_s, row_r).wait_send()

    each(n_seq, sent_all, 1)
    slot_at = iota_f((slots, count), 0)

    def return_group(g):
        p0 = group_out(g)
        hot = ones_where(slot_at == srow[0:1, :] - (p0 * cap).astype(f32)).astype(bf16)
        made = mm(hot, val_hi[...]) + mm(hot, val_lo[...])
        outb[pl.ds(p0, group)] = made.reshape(group, cap, chans)
        launch(p0, inb2, back_s, back_r)

    if spare:
        hot = ones_where(
            jnp.broadcast_to(orow[0:1, :], (n_seq, count)) == iota_f((n_seq, count), 0)).astype(bf16)
        hop_send(mm(hot, val_hi[...]) + mm(hot, val_lo[...]), *ret1)
        each(n_groups // 2, return_group)
        high, low = hop_read(*ret1)
        hop_send(mm_first(pass_on, high) + mm_first(pass_on, low), *ret2)
        each(n_groups, return_group, n_groups // 2)
    else:
        each(n_groups, return_group)

    for d in range(2 * half + 1):
        small[d:d + 1, :] = jnp.sum(gtap_acc[d], axis=0, keepdims=True)
    small[7:8, :] = mgain_part
    small[8:16, :] = jnp.broadcast_to(misfit, (8, chans))
    rs1[dp] = small[...]

    def s1_send(o):
        to = lax.rem(dp + o, n_dp)
        return remote(small, rs1.at[dp], s1_s.at[to], s1_r.at[dp], to, me)

    def s1_recv(o):
        to = lax.rem(dp + o, n_dp)
        return remote(small, rs1.at[to], s1_s.at[to], s1_r.at[to], to, me)

    each(n_dp, lambda o: s1_send(o).start(), 1)

    mixed_v[...] += sum(
        mm(rows_hl[j * segs:(j + 1) * segs, :], wout_v[j * hb:(j + 1) * hb, :]) for j in range(n_hb))
    store_mixed = pltpu.make_async_copy(mixed_v, mixed_hbm, ld_sem.at[4])
    store_mixed.start()

    share = hidden // n_seq
    z_per = n_z // n_hb

    def x_send(j, o):
        xx = lax.rem(x + o, NX)
        at, k = pl.ds(j * z_per, z_per), j * NX + o - 1
        return remote(wx.at[xx, at], rx.at[o - 1, at], x_s.at[k], x_r.at[k], dp, z * NX + xx)

    def y_done(j):
        each(n_y, lambda o: y_send(j, o).wait_recv(), 1)

        def add_y(i):
            zz, xx = j * z_per + lax.div(i, NX), lax.rem(i, NX)
            at = pl.ds(pl.multiple_of((zz * NX + xx) * share, share), share)
            total = gw[core, y, at, :]
            for o in range(n_y - 1):
                total = total + ry[o, at, :]
            wx[xx, zz] = total

        each(z_per * NX, add_y)
        each(NX, lambda o: x_send(j, o).start(), 1)

    each(n_hb, y_done)
    each(n_dp, lambda o: s1_recv(o).wait_recv(), 1)
    total = rs1[0]
    for i in range(1, n_dp):
        total = total + rs1[i]
    rs2[x] = total

    def s2_send(o):
        xx = lax.rem(x + o, NX)
        return remote(rs2.at[x], rs2.at[x], s2_s.at[xx], s2_r.at[x], dp, z * NX + xx)

    def s2_recv(o):
        xx = lax.rem(x + o, NX)
        return remote(rs2.at[x], rs2.at[xx], s2_s.at[xx], s2_r.at[xx], dp, z * NX + xx)

    each(NX, lambda o: s2_send(o).start(), 1)
    each(n_hb, lambda j: each(NX, lambda o: x_send(j, o).wait_recv(), 1))

    def add_x(zz):
        total = wx[x, zz]
        for o in range(NX - 1):
            total = total + rx[o, zz]
        wz[zz] = total

    each(n_z, add_x)
    each(NX, lambda o: s2_recv(o).wait_recv(), 1)
    total = rs2[0]
    for i in range(1, NX):
        total = total + rs2[i]
    rs3[z] = total

    def z_send(o):
        zz = lax.rem(z + o, n_z)
        return remote(wz.at[zz], rz.at[o - 1], z_s.at[o - 1], z_r.at[o - 1], dp, zz * NX + x)

    def s3_send(o):
        zz = lax.rem(z + o, n_z)
        return remote(rs3.at[z], rs3.at[z], s3_s.at[zz], s3_r.at[z], dp, zz * NX + x)

    def s3_recv(o):
        zz = lax.rem(z + o, n_z)
        return remote(rs3.at[z], rs3.at[zz], s3_s.at[zz], s3_r.at[zz], dp, zz * NX + x)

    each(n_z, lambda o: z_send(o).start(), 1)
    each(n_z, lambda o: s3_send(o).start(), 1)
    each(n_z, lambda o: z_send(o).wait_recv(), 1)
    total = wz[z]
    for o in range(n_z - 1):
        total = total + rz[o]
    fin[core, y] = total

    def f_send(o):
        to = lax.rem(dp + o, n_dp)
        return remote(fin.at[core, y], fin.at[core, y], f_s.at[to], f_r.at[dp], to, me)

    def f_recv(o):
        to = lax.rem(dp + o, n_dp)
        part = fin.at[lax.rem(to, 2), lax.div(to, 2)]
        return remote(fin.at[core, y], part, f_s.at[to], f_r.at[to], to, me)

    each(n_dp, lambda o: f_send(o).start(), 1)
    each(n_z, lambda o: s3_recv(o).wait_recv(), 1)
    total = rs3[0]
    for i in range(1, n_z):
        total = total + rs3[i]
    gtaps_ref[...] = total[0:2 * half + 1, :] * cgain
    gcg_ref[...] = jnp.sum(total[0:2 * half + 1, :] * taps, axis=0, keepdims=True)
    gmg_ref[...] = total[7:8, :]
    misfit_ref[...] = total[8:16, 0:128]

    def clear_rows(i):
        rows_v[pl.ds(pl.multiple_of(i * 8, 8), 8), :] = jnp.zeros((8, chans), f32)

    each(count // 8, clear_rows)

    def settle_group(g):
        p0 = group_in(g)
        arrive(p0, inb2, back_s, back_r)
        high, low = split_hi_lo(inb2[pl.ds(p0, group)].reshape(slots, chans))
        hot = pick[pl.ds(pl.multiple_of(p0 * cap, 16), slots), :]
        rows_v[...] += mm_first(hot, high) + mm_first(hot, low)

    each(n_groups, settle_group)
    if spare:
        high, low = hop_read(*ret2)
        rows_v[...] += mm_first(pick2[...], high) + mm_first(pick2[...], low)
    store_rows = pltpu.make_async_copy(rows_v, grows_hbm, ld_sem.at[5])
    store_rows.start()

    each(n_dp, lambda o: f_recv(o).wait_recv(), 1)
    gwout_ref[...] = jnp.concatenate([fin[1, c] for c in range(n_cols)], axis=1)
    gwin_ref[...] = jnp.concatenate([fin[0, c] for c in range(n_cols)], axis=1)

    each(n_seq, lambda i: send_list(i).wait_send(), 1)

    def back_sent(i):
        p = lax.rem(me + i, n_seq)
        row_out(p, outb, inb2, back_s, back_r).wait_send()

    each(n_seq, back_sent, 1)
    for copy in halo(ser, 0) + halo(gc, 2):
        copy.wait_send()
    each(n_hb, lambda j: core_copy(j).wait_send())
    each(n_hb, lambda j: each(n_y, lambda o: y_send(j, o).wait_send(), 1))
    each(n_hb, lambda j: each(NX, lambda o: x_send(j, o).wait_send(), 1))
    each(n_z, lambda o: z_send(o).wait_send(), 1)
    each(n_dp, lambda o: s1_send(o).wait_send(), 1)
    each(NX, lambda o: s2_send(o).wait_send(), 1)
    each(n_z, lambda o: s3_send(o).wait_send(), 1)
    each(n_dp, lambda o: f_send(o).wait_send(), 1)
    if spare:
        for hop in (hop1, hop2, ret1, ret2):
            each(n_seq, lambda i: hop_out(i, *hop).wait_send(), 1)
    store_mixed.wait()
    store_rows.wait()


def copy_out(*refs):
    count = len(refs) // 2
    for src, dst in zip(refs[:count], refs[count:]):
        dst[...] = src[...]


def make_body(n_dp, n_seq):
    n_y, n_z = n_dp // 2, n_seq // NX

    def body(point_rows, serial_order, scene_counts, pool_counts, conv_gain, conv_kernel, mixer_gain,
             weight_in, weight_out, grad_out):
        count, chans = point_rows.shape
        segs = grad_out.shape[0]
        hidden = weight_out.shape[0]
        even = count // n_seq
        share = hidden // n_seq
        pads = count + 2 * PAD
        cols = chans // 128
        V = pltpu.VMEM
        D = lambda n: pltpu.SemaphoreType.DMA((n,))
        any_spec = pl.BlockSpec(memory_space=pl.ANY)
        vmem = pl.BlockSpec(memory_space=pltpu.VMEM)
        shape = jax.ShapeDtypeStruct
        scratch = lambda cap: [
            V((count, chans), f32), V((2 * count, chans), bf16),
            V((n_seq, 8, 128), f32), V((n_seq, 8, 128), f32), V((count, 128), bf16),
            V((count, 128), f32), V((8, count), f32), V((128, n_seq * 8), f32), V((n_seq * cap, count), bf16),
            V((n_seq, cap, chans), f32), V((n_seq, cap, chans), f32), V((n_seq, cap, chans), f32),
            V((pads, chans), f32), V((pads, chans), f32), V((pads, 128), f32), V((pads, 128), f32),
            V((2 * count, chans), bf16),
            V((segs, count), bf16), V((count, segs), bf16), V((segs, 128), f32),
            V((segs, chans), f32), V((segs, chans), bf16), V((segs, chans), f32), V((segs, chans), f32),
            V((segs, chans), bf16), V((segs, chans), f32), V((segs, 128), f32),
            V((chans, hidden), bf16), V((hidden, chans), bf16),
            V((2, cols, hidden, 128), f32), V((cols, hidden, 128), f32), V((n_y - 1, hidden, 128), f32),
            V((NX, n_z, share, 128), f32), V((NX - 1, n_z, share, 128), f32),
            V((n_z, share, 128), f32), V((n_z - 1, share, 128), f32), V((2, cols, share, 128), f32),
            V((pads, chans), f32), V((8, 8, chans), f32), V((16, chans), f32),
            V((n_dp, 16, chans), f32), V((NX, 16, chans), f32), V((n_z, 16, chans), f32),
            D(6), D(n_seq), D(n_seq), D(n_seq), D(n_seq), D(n_seq), D(n_seq), D(4), D(4),
            D(hidden // 512), D(hidden // 512), D(4 * n_y), D(4 * n_y), D(4 * NX), D(4 * NX), D(n_z), D(n_z),
            D(n_dp), D(n_dp), D(NX), D(NX), D(n_z), D(n_z), D(n_dp), D(n_dp),
        ]
        hop = [V((n_seq, 1, chans), f32)] * 8
        extra = [V((count, 128), f32), V((8, count), f32), V((n_seq, count), bf16)] + hop + [D(n_seq)] * 8

        def call(cap, spare, ident, name):
            return pl.pallas_call(
                lambda *refs: kernel(n_dp, n_seq, cap, spare, *refs),
                out_shape=(
                    shape((segs, chans), f32), shape((count, chans), f32), shape((share, chans), f32),
                    shape((share, chans), f32), shape(conv_kernel.shape, f32), shape((1, chans), f32),
                    shape((1, chans), f32), shape((8, 128), f32),
                ),
                in_specs=[any_spec] + [vmem] * 6 + [any_spec] * 3,
                out_specs=(any_spec, any_spec, vmem, vmem, vmem, vmem, vmem, vmem),
                scratch_shapes=scratch(cap) + (extra if spare else []),
                compiler_params=pltpu.CompilerParams(
                    collective_id=ident, has_side_effects=True, vmem_limit_bytes=62 * 1024 * 1024),
                name=name,
            )(
                point_rows, serial_order, scene_counts, pool_counts.reshape(1, segs), conv_gain[None], conv_kernel,
                mixer_gain[None], weight_in, weight_out, grad_out,
            )

        outs = call(even, even // 2, 0, "window_even")
        outs = lax.cond(
            outs[7][0, 0] > 0.0, lambda: call(even + even // 2, 0, 1, "window_full")[:7], lambda: outs[:7])
        steps = 4
        specs = tuple(
            pl.BlockSpec((value.shape[0] // steps, value.shape[1]), lambda i: (i, 0)) if k < 2
            else pl.BlockSpec(value.shape, lambda i: (0, 0)) for k, value in enumerate(outs))
        mixed, grows, gwin, gwout, gtaps, gcg, gmg = pl.pallas_call(
            copy_out,
            out_shape=tuple(shape(value.shape, f32) for value in outs),
            grid=(steps,),
            in_specs=list(specs),
            out_specs=specs,
            name="outputs",
        )(*outs)
        return mixed, grows, gwin.T, gwout, gtaps, gcg[0], gmg[0]

    return body


def solution(mesh):
    return jax.shard_map(
        make_body(mesh.shape["dp"], mesh.shape["seq"]),
        mesh=mesh,
        in_specs=(
            P(("dp", "seq"), None), P("dp", "seq"), P("dp", None), P("dp", "seq", None), P(), P(), P(), P(), P(),
            P(("dp", "seq"), None),
        ),
        out_specs=(
            P(("dp", "seq"), None), P(("dp", "seq"), None), P(None, "seq"), P("seq", None), P(), P(), P(),
        ),
        check_vma=False,
    )
```
